512 devices in a mesh: section: 8 (over x, core), dp: 64 (over y, z).
Axes of the slice: x: 4, y: 8, z: 8, core: 2. Of those that a mesh axis runs over, the one named last changes fastest.
Arguments:
- hidden_in: bfloat16 [64, 192, 1024], P('dp'), may hold values from -6 to 6
- cotangent: bfloat16 [64, 192, 1024], P('dp'), may hold values from -0.15625 to 0.15625
- segments: int32 [64, 192], P('dp'), may hold values from 0 to 23, never falling along the last dimension, each value on 1 to 48 neighbouring positions
- attn_weights: bfloat16 [8, 3, 1024, 1024], P('section', None, 'dp'), may hold values from -8 to 8
- out_weight: bfloat16 [8, 1024, 1024], P('section', 'dp'), may hold values from -0.1875 to 0.1875
Outputs:
- grad_out: float32 [8, 1024, 1024], P('section', 'dp')
The draws below stay inside these ranges and needn't reach their ends.
Inputs may be any that keep to these rules, and one draw needn't show every extreme that they name: `segments`: along each context the ids never fall, each id from 0 to 23 occurs and covers 1 to 48 positions, one of them exactly 48.
All inputs are finite; a program needn't handle non-finite values.
Results may differ from the reference program's by a relative error of at most 0.029.
Values may be sent and summed in bfloat16 or wider, within the bound.
A program may use at most 64 MiB of HBM per device.

```python
import math
import jax
import jax.numpy as jnp
import numpy as np
from jax import lax

HEADS = 16
HEAD_DIM = 64
D = 1024
L = 192
LAYERS = 8
CONTEXTS = 64


def draw_attn_weights(key, part):
    key = jax.random.fold_in(key, 3)
    sample = jax.random.normal(key, (LAYERS, 3, D, D), jnp.float32) * D ** (-0.5)
    return jnp.clip(sample, -8.0, 8.0).astype(jnp.bfloat16)


def raised(entries, rng, source, target, parts, factor):
    def block_of(axis_at):
        return (jnp.arange(entries.shape[axis_at]) // (entries.shape[axis_at] // parts)).reshape((-1,) + (1,) * (entries.ndim - 1 - axis_at))

    one_side = jax.random.permutation(rng, parts)[block_of(target)]
    far = (block_of(target) + parts // 2) % parts
    return jnp.where((block_of(source) == one_side) | (block_of(source) == far), factor * entries, entries)


def block_scale(own_key, dims, cuts, low, high):
    def one(dim, parts):
        draws = jax.random.uniform(jax.random.fold_in(jax.random.fold_in(own_key, 6), dim), (parts,), jnp.float32, low / len(cuts), high / len(cuts))
        return jnp.repeat(jnp.exp(draws), dims[dim] // parts).reshape((-1,) + (1,) * (len(dims) - dim - 1))

    factor_of = one(*cuts[0])
    for cut in cuts[1:]:
        factor_of = factor_of * one(*cut)
    return factor_of


def length_profile(number_of, total, limit, skew):
    weights = [(1 << 20) // math.isqrt(rank ** skew) + 1 for rank in range(2, number_of + 1)]
    surplus, given = total - limit - (number_of - 1), [1] * (number_of - 1)
    while surplus > 0:
        candidates = [i for i in range(number_of - 1) if given[i] < limit]
        mass, remaining = sum([weights[i] for i in candidates]), surplus
        for i in candidates:
            addition = min(limit - given[i], max(1, remaining * weights[i] // mass), surplus)
            given[i] = given[i] + addition
            surplus = surplus - addition
    return np.array([limit] + given)


def uneven(rng, number_of, total, limit, slope):
    if number_of == 2:
        one = jax.random.randint(rng, (), max(1, total - limit), min(limit, total - 1) + 1)
        return jnp.stack([one, total - one])
    tallies = jnp.asarray(length_profile(number_of, total, limit, slope), jnp.int32)
    couples = (number_of - 1) // 2
    donor, sink = tallies[1:1 + 2 * couples:2], tallies[2:2 + 2 * couples:2]
    slack = jnp.minimum(donor - 1, limit - sink)
    shifted = jax.random.randint(jax.random.fold_in(rng, 1), (couples,), 0, 1 << 20) % (slack + 1)
    tallies = tallies.at[1:1 + 2 * couples:2].set(donor - shifted).at[2:2 + 2 * couples:2].set(sink + shifted)
    return tallies[jax.random.permutation(jax.random.fold_in(rng, 2), number_of)]


def normal_values(stream_key, shape, width, limit, shards=(), kind=jnp.bfloat16):
    result = width * jax.random.normal(stream_key, shape, jnp.float32)
    if shards:
        result = result * block_scale(stream_key, shape, shards, -0.22, 0.18)
    return jnp.clip(result, -limit, limit).astype(kind)


def bell_draw_with(own_key, shape, scale, bound, pieces, heavy, kind=jnp.bfloat16):
    values = scale * jax.random.normal(own_key, shape, jnp.float32)
    if pieces:
        values = values * block_scale(own_key, shape, pieces, -0.22, 0.18)
    return jnp.clip(raised(values, jax.random.fold_in(own_key, 3), *heavy), -bound, bound).astype(kind)


def setup_inputs(seed: int = 0) -> dict:
    arg_keys = jax.random.split(jax.random.key(seed), 6)
    hidden_in = normal_values(arg_keys[0], (CONTEXTS, L, D), 1.0, 6.0, ((0, 64),))
    cotangent = bell_draw_with(arg_keys[1], (CONTEXTS, L, D), ((CONTEXTS * L) ** -0.5), 0.15625, ((0, 64),), (0, 2, 64, 4.0))
    segments = jax.vmap(lambda own: jnp.searchsorted(jnp.cumsum(uneven(own, L // 8, L, L // 4, 1)), jnp.arange(L), side="right"))(jax.random.split(arg_keys[2], CONTEXTS)).reshape((CONTEXTS, L)).astype(jnp.int32)
    attn_weights = draw_attn_weights(jax.random.fold_in(arg_keys[5], 71), 0)
    out_weight = normal_values(arg_keys[4], (LAYERS, D, D), D ** -0.5, 0.1875, ((0, 8), (1, 64)))
    return dict(hidden_in=hidden_in, cotangent=cotangent, segments=segments, attn_weights=attn_weights, out_weight=out_weight)


epsilon = 1e-05
masked_score = -1e+30

def normalize(hidden):
    widened = hidden.astype(jnp.float32)
    row_scale = lax.rsqrt(lax.optimization_barrier(jnp.mean(widened * widened, axis=-1, keepdims=True)) + epsilon)
    return (widened * row_scale).astype(jnp.bfloat16)

def project(normed, weight):
    return jnp.dot(normed, weight.T, preferred_element_type=jnp.float32).astype(jnp.bfloat16)

def attend(queries, key_rows, values, allowed):
    query_count = queries.shape[0]
    key_count = key_rows.shape[0]
    query_heads = queries.astype(jnp.float32).reshape(query_count, HEADS, HEAD_DIM)
    key_heads = key_rows.astype(jnp.float32).reshape(key_count, HEADS, HEAD_DIM)
    value_heads = values.astype(jnp.float32).reshape(key_count, HEADS, HEAD_DIM)
    scores = jnp.einsum('qhd,khd->hqk', query_heads, key_heads) * HEAD_DIM ** (-0.5)
    scores = jnp.where(allowed[None], scores, masked_score)
    weights = jax.nn.softmax(scores, axis=-1).astype(jnp.bfloat16)
    mixed_heads = jnp.einsum('hqk,khd->qhd', weights.astype(jnp.float32), value_heads)
    return mixed_heads.reshape(query_count, HEADS * HEAD_DIM).astype(jnp.bfloat16)

def apply_layer(hidden, allowed, attn_layer, out_layer):
    normed = normalize(hidden)
    queries = project(normed, attn_layer[0])
    key_rows = project(normed, attn_layer[1])
    values = project(normed, attn_layer[2])
    mixed_heads = attend(queries, key_rows, values, allowed)
    added = hidden.astype(jnp.float32) + jnp.dot(mixed_heads, out_layer.T, preferred_element_type=jnp.float32)
    return added.astype(jnp.bfloat16)

def reference(hidden_in, cotangent, segments, attn_weights, out_weight):
    positions = jnp.arange(L, dtype=jnp.int32)
    causal = positions[None, :] <= positions[:, None]

    def per_context(totals, item):
        context, context_cot, context_seg = item
        same_segment = context_seg[:, None] == context_seg[None, :]

        def run_layers(out_stack):
            hidden = context
            for layer_index in range(LAYERS):
                if layer_index % 2 == 0:
                    allowed = causal & same_segment
                else:
                    allowed = causal
                hidden = apply_layer(hidden, allowed, attn_weights[layer_index], out_stack[layer_index])
            return hidden
        unused_out, pullback = jax.vjp(run_layers, out_weight)
        grad_o = pullback(context_cot)[0]
        return (totals + grad_o.astype(jnp.float32), None)
    start = jnp.zeros(out_weight.shape, jnp.float32)
    totals, unused_stack = lax.scan(per_context, start, (hidden_in, cotangent, segments))
    return totals
```

```python
import functools
import jax
import jax.numpy as jnp
from jax import lax
from jax.experimental import pallas as pl
from jax.experimental.pallas import tpu as pltpu
from jax.sharding import PartitionSpec as P

MESH = pl.DeviceIdType.MESH
HEADS = 16
HEAD_DIM = 64
PAIRS = HEADS // 2
PAIR = 2 * HEAD_DIM
NC = 2
SECTIONS = 8
epsilon = 1e-05
masked_score = -1e30

NT = (((1,), (1,)), ((), ()))
NN = (((1,), (0,)), ((), ()))
TN = (((0,), (0,)), ((), ()))


def dot(a, b, dims):
    return lax.dot_general(a, b, dims, preferred_element_type=jnp.float32)


def halves(block, low):
    zero = jnp.zeros_like(block)
    return jnp.concatenate([jnp.where(low, block, zero), jnp.where(low, zero, block)], axis=0)


def pipeline_kernel(
    x_ref, cot_ref, bias_ref, w_ref, dw_ref,
    hid, outb, gin, gout, qb, kb, vb, mixb, pb, dmb, dqb, dkb, dvb,
    fsend, frecv, bsend, brecv,
):
    s = lax.axis_index("section")
    length, width = x_ref.shape
    rows_c = length // NC
    barrier = pltpu.get_barrier_semaphore()

    for step in (1, SECTIONS - 1):
        other = lax.rem(s + step, SECTIONS)
        pl.semaphore_signal(barrier, inc=1, device_id={"section": other}, device_id_type=MESH)
    pl.semaphore_wait(barrier, 2)

    def forward_copy(c):
        rows = pl.ds(c * rows_c, rows_c)
        return pltpu.make_async_remote_copy(
            src_ref=outb.at[rows], dst_ref=hid.at[rows], send_sem=fsend.at[c], recv_sem=frecv.at[c],
            device_id={"section": jnp.minimum(s + 1, SECTIONS - 1)}, device_id_type=MESH,
        )

    def backward_copy(c):
        rows = pl.ds(c * rows_c, rows_c)
        return pltpu.make_async_remote_copy(
            src_ref=gout.at[rows], dst_ref=gin.at[rows], send_sem=bsend.at[c], recv_sem=brecv.at[c],
            device_id={"section": jnp.maximum(s - 1, 0)}, device_id_type=MESH,
        )

    @pl.when(s == 0)
    def _():
        hid[...] = x_ref[...]

    @pl.when(s == SECTIONS - 1)
    def _():
        gin[...] = cot_ref[...]

    dkb[...] = jnp.zeros_like(dkb)
    dvb[...] = jnp.zeros_like(dvb)
    low = lax.broadcasted_iota(jnp.int32, (rows_c, PAIR), 1) < HEAD_DIM

    for c in range(NC):
        lo, hi = c * rows_c, (c + 1) * rows_c

        @pl.when(s > 0)
        def _():
            forward_copy(c).wait_recv()

        h = hid[lo:hi].astype(jnp.float32)
        r = lax.rsqrt(jnp.mean(h * h, axis=-1, keepdims=True) + epsilon)
        normed = (h * r).astype(jnp.bfloat16)
        for j, buf in ((0, qb), (1, kb), (2, vb)):
            buf[lo:hi] = dot(normed, w_ref[j], NT).astype(jnp.bfloat16)
        bias = bias_ref[lo:hi, :hi]
        bias2 = jnp.concatenate([bias, bias], axis=0)
        for p in range(PAIRS):
            cols = slice(p * PAIR, (p + 1) * PAIR)
            q01 = halves(qb[lo:hi, cols], low)
            scores = dot(q01, kb[:hi, cols], NT) * HEAD_DIM ** (-0.5) + bias2
            top = jnp.max(scores, axis=-1, keepdims=True)
            e = jnp.exp(scores - top)
            weights = (e / jnp.sum(e, axis=-1, keepdims=True)).astype(jnp.bfloat16)
            pb[c, p, :, :hi] = weights
            o = dot(weights, vb[:hi, cols], NN)
            mixb[lo:hi, cols] = jnp.where(low, o[:rows_c], o[rows_c:]).astype(jnp.bfloat16)

        @pl.when(s < SECTIONS - 1)
        def _():
            added = hid[lo:hi].astype(jnp.float32) + dot(mixb[lo:hi], w_ref[3], NT)
            outb[lo:hi] = added.astype(jnp.bfloat16)
            forward_copy(c).start()

    for c in reversed(range(NC)):
        lo, hi = c * rows_c, (c + 1) * rows_c

        @pl.when(s < SECTIONS - 1)
        def _():
            backward_copy(c).wait_recv()

        @pl.when(s > 0)
        def _():
            g = gin[lo:hi]
            dmb[...] = dot(g, w_ref[3], NN).astype(jnp.bfloat16)
            for p in range(PAIRS):
                cols = slice(p * PAIR, (p + 1) * PAIR)
                d01 = halves(dmb[:, cols], low)
                q01 = halves(qb[lo:hi, cols], low)
                weights = pb[c, p, :, :hi]
                wide = weights.astype(jnp.float32)
                dweights = dot(d01, vb[:hi, cols], NT)
                delta = jnp.sum(wide * dweights, axis=-1, keepdims=True)
                ds = (wide * (dweights - delta) * HEAD_DIM ** (-0.5)).astype(jnp.bfloat16)
                dq01 = dot(ds, kb[:hi, cols], NN)
                dqb[:, cols] = jnp.where(low, dq01[:rows_c], dq01[rows_c:]).astype(jnp.bfloat16)
                dkb[:hi, cols] += dot(ds, q01, TN)
                dvb[:hi, cols] += dot(weights, d01, TN)
            dn = dot(dqb[...], w_ref[0], NN)
            dn += dot(dkb[lo:hi].astype(jnp.bfloat16), w_ref[1], NN)
            dn += dot(dvb[lo:hi].astype(jnp.bfloat16), w_ref[2], NN)
            h = hid[lo:hi].astype(jnp.float32)
            r = lax.rsqrt(jnp.mean(h * h, axis=-1, keepdims=True) + epsilon)
            along = jnp.mean(dn * h, axis=-1, keepdims=True)
            dh = dn * r - h * (r * r * r * along)
            gout[lo:hi] = (g.astype(jnp.float32) + dh).astype(jnp.bfloat16)
            backward_copy(c).start()

    step = 256
    for j in range(0, width, step):
        dw_ref[j : j + step] = dot(gin[:, j : j + step], mixb[...], TN).astype(jnp.bfloat16)

    for c in range(NC):
        @pl.when(s < SECTIONS - 1)
        def _():
            forward_copy(c).wait_send()

        @pl.when(s > 0)
        def _():
            backward_copy(c).wait_send()


def pipeline(context, cot, bias, weights):
    length, width = context.shape
    rows_c = length // NC
    full = pltpu.VMEM((length, width), jnp.bfloat16)
    return pl.pallas_call(
        pipeline_kernel,
        name="pipeline",
        out_shape=jax.ShapeDtypeStruct((width, width), jnp.bfloat16),
        in_specs=[pl.BlockSpec(memory_space=pltpu.VMEM)] * 4,
        out_specs=pl.BlockSpec(memory_space=pltpu.VMEM),
        scratch_shapes=[full] * 8 + [
            pltpu.VMEM((NC, PAIRS, 2 * rows_c, length), jnp.bfloat16),
            pltpu.VMEM((rows_c, width), jnp.bfloat16),
            pltpu.VMEM((rows_c, width), jnp.bfloat16),
            pltpu.VMEM((length, width), jnp.float32),
            pltpu.VMEM((length, width), jnp.float32),
        ] + [pltpu.SemaphoreType.DMA((NC,))] * 4,
        compiler_params=pltpu.CompilerParams(
            collective_id=1, has_side_effects=True, vmem_limit_bytes=48 << 20
        ),
    )(context, cot, bias, weights)


def local(hidden_in, cotangent, segments, attn_weights, out_weight):
    width = out_weight.shape[-1]
    section_index = lax.axis_index("section")
    shard = jnp.concatenate([attn_weights[0], out_weight], axis=0)
    weights = lax.all_gather(shard, "dp", axis=1, tiled=True)
    context = hidden_in[0]
    length = context.shape[0]
    positions = jnp.arange(length, dtype=jnp.int32)
    causal = positions[None, :] <= positions[:, None]
    same_segment = segments[0][:, None] == segments[0][None, :]
    allowed = causal & (same_segment | (section_index % 2 == 1))
    bias = jnp.where(allowed, 0.0, masked_score).astype(jnp.float32)
    grad = pipeline(context, cotangent[0], bias, weights)
    result = lax.psum_scatter(grad.astype(jnp.float32), "dp", scatter_dimension=0, tiled=True)
    return result[None]


def solution(mesh):
    in_specs = (
        P("dp", None, None),
        P("dp", None, None),
        P("dp", None),
        P("section", None, "dp", None),
        P("section", "dp", None),
    )
    return jax.shard_map(
        local, mesh=mesh, in_specs=in_specs, out_specs=P("section", "dp", None), check_vma=False
    )
```

```python
import functools
import jax
import jax.numpy as jnp
from jax import lax
from jax.experimental import pallas as pl
from jax.experimental.pallas import tpu as pltpu
from jax.sharding import PartitionSpec as P

MESH = pl.DeviceIdType.MESH
HEADS = 16
HEAD_DIM = 64
PAIRS = HEADS // 2
PAIR = 2 * HEAD_DIM
NC = 2
SECTIONS = 8
RING = 8
epsilon = 1e-05
masked_score = -1e30

NT = (((1,), (1,)), ((), ()))
NN = (((1,), (0,)), ((), ()))
TN = (((0,), (0,)), ((), ()))


def dot(a, b, dims):
    return lax.dot_general(a, b, dims, preferred_element_type=jnp.float32)


def halves(block, low):
    zero = jnp.zeros_like(block)
    return jnp.concatenate([jnp.where(low, block, zero), jnp.where(low, zero, block)], axis=0)


def gather_copy(w_ref, sends, recvs, phase, j, way, step):
    d = lax.axis_index("dp")
    y, z = d // RING, lax.rem(d, RING)
    along_z = (j < 2) == (phase == 0)
    me = z if along_z else y
    block = lax.rem(me - way * (step - 1) + RING, RING)
    other = lax.rem(me + way + RING, RING)
    other = y * RING + other if along_z else other * RING + z
    if phase == 0:
        ref = w_ref.at[j, y, block] if along_z else w_ref.at[j, block, z]
    else:
        ref = w_ref.at[j, :, block] if along_z else w_ref.at[j, block]
    bit = (1 - way) // 2
    return pltpu.make_async_remote_copy(
        src_ref=ref, dst_ref=ref, send_sem=sends.at[phase, j, bit, step - 1],
        recv_sem=recvs.at[phase, j, bit, step - 1], device_id={"dp": other}, device_id_type=MESH,
    )


def gather_steps(j, way):
    return RING // 2 if (way == 1) == (j % 2 == 0) else RING // 2 - 1


STREAMS = [(j, way) for j in range(4) for way in (1, -1)]


def gather(w_ref, sends, recvs):
    for phase in range(2):
        for j, way in STREAMS:
            gather_copy(w_ref, sends, recvs, phase, j, way, 1).start()
        for step in range(1, RING // 2 + 1):
            for j, way in STREAMS:
                if step <= gather_steps(j, way):
                    gather_copy(w_ref, sends, recvs, phase, j, way, step).wait_recv()
                if step < gather_steps(j, way):
                    gather_copy(w_ref, sends, recvs, phase, j, way, step + 1).start()


def gather_end(w_ref, sends, recvs):
    for phase in range(2):
        for j, way in STREAMS:
            for step in range(1, gather_steps(j, way) + 1):
                gather_copy(w_ref, sends, recvs, phase, j, way, step).wait_send()


ORDER = (4, 3, 5, 2, 6, 1, 7)


def scatter_copy(src, dst, send, recv, along_z, k):
    d = lax.axis_index("dp")
    y, z = d // RING, lax.rem(d, RING)
    place = lax.rem((z if along_z else y) + k, RING)
    other = y * RING + place if along_z else place * RING + z
    return pltpu.make_async_remote_copy(
        src_ref=src(place), dst_ref=dst.at[k - 1], send_sem=send.at[k - 1], recv_sem=recv.at[k - 1],
        device_id={"dp": other}, device_id_type=MESH,
    )


def pipeline_kernel(
    x_ref, cot_ref, bias_ref, attn_ref, out_ref, o_ref,
    w_ref, dw, landa, landb, parta, partb, enda, endb,
    gsend, grecv, rsend, rrecv,
    hid, outb, gin, gout, qb, kb, vb, mixb, pb, dmb, dqb, dkb, dvb,
    fsend, frecv, bsend, brecv,
):
    s = lax.axis_index("section")
    length, width = x_ref.shape
    rows_c = length // NC
    barrier = pltpu.get_barrier_semaphore()

    d = lax.axis_index("dp")
    y, z = d // RING, lax.rem(d, RING)
    for step in (1, SECTIONS - 1):
        other = lax.rem(s + step, SECTIONS)
        pl.semaphore_signal(barrier, inc=1, device_id={"section": other}, device_id_type=MESH)
    for step in range(1, RING):
        for other in (lax.rem(y + step, RING) * RING + z, y * RING + lax.rem(z + step, RING)):
            pl.semaphore_signal(barrier, inc=1, device_id={"dp": other}, device_id_type=MESH)
    for j in range(3):
        w_ref[j, y, z] = attn_ref[j]
    w_ref[3, y, z] = out_ref[...]
    pl.semaphore_wait(barrier, 2 + 2 * (RING - 1))
    gather(w_ref, gsend, grecv)
    weight = lambda j: w_ref[j].reshape(width, width)

    def forward_copy(c):
        rows = pl.ds(c * rows_c, rows_c)
        return pltpu.make_async_remote_copy(
            src_ref=outb.at[rows], dst_ref=hid.at[rows], send_sem=fsend.at[c], recv_sem=frecv.at[c],
            device_id={"section": jnp.minimum(s + 1, SECTIONS - 1)}, device_id_type=MESH,
        )

    def backward_copy(c):
        rows = pl.ds(c * rows_c, rows_c)
        return pltpu.make_async_remote_copy(
            src_ref=gout.at[rows], dst_ref=gin.at[rows], send_sem=bsend.at[c], recv_sem=brecv.at[c],
            device_id={"section": jnp.maximum(s - 1, 0)}, device_id_type=MESH,
        )

    @pl.when(s == 0)
    def _():
        hid[...] = x_ref[...]

    @pl.when(s == SECTIONS - 1)
    def _():
        gin[...] = cot_ref[...]

    dkb[...] = jnp.zeros_like(dkb)
    dvb[...] = jnp.zeros_like(dvb)
    low = lax.broadcasted_iota(jnp.int32, (rows_c, PAIR), 1) < HEAD_DIM

    for c in range(NC):
        lo, hi = c * rows_c, (c + 1) * rows_c

        @pl.when(s > 0)
        def _():
            forward_copy(c).wait_recv()

        h = hid[lo:hi].astype(jnp.float32)
        r = lax.rsqrt(jnp.mean(h * h, axis=-1, keepdims=True) + epsilon)
        normed = (h * r).astype(jnp.bfloat16)
        for j, buf in ((0, qb), (1, kb), (2, vb)):
            buf[lo:hi] = dot(normed, weight(j), NT).astype(jnp.bfloat16)
        bias = bias_ref[lo:hi, :hi]
        bias2 = jnp.concatenate([bias, bias], axis=0)
        for p in range(PAIRS):
            cols = slice(p * PAIR, (p + 1) * PAIR)
            q01 = halves(qb[lo:hi, cols], low)
            scores = dot(q01, kb[:hi, cols], NT) * HEAD_DIM ** (-0.5) + bias2
            top = jnp.max(scores, axis=-1, keepdims=True)
            e = jnp.exp(scores - top)
            weights = (e / jnp.sum(e, axis=-1, keepdims=True)).astype(jnp.bfloat16)
            pb[c, p, :, :hi] = weights
            o = dot(weights, vb[:hi, cols], NN)
            mixb[lo:hi, cols] = jnp.where(low, o[:rows_c], o[rows_c:]).astype(jnp.bfloat16)

        @pl.when(s < SECTIONS - 1)
        def _():
            added = hid[lo:hi].astype(jnp.float32) + dot(mixb[lo:hi], weight(3), NT)
            outb[lo:hi] = added.astype(jnp.bfloat16)
            forward_copy(c).start()

    for c in reversed(range(NC)):
        lo, hi = c * rows_c, (c + 1) * rows_c

        @pl.when(s < SECTIONS - 1)
        def _():
            backward_copy(c).wait_recv()

        @pl.when(s > 0)
        def _():
            g = gin[lo:hi]
            dmb[...] = dot(g, weight(3), NN).astype(jnp.bfloat16)
            for p in range(PAIRS):
                cols = slice(p * PAIR, (p + 1) * PAIR)
                d01 = halves(dmb[:, cols], low)
                q01 = halves(qb[lo:hi, cols], low)
                weights = pb[c, p, :, :hi]
                wide = weights.astype(jnp.float32)
                dweights = dot(d01, vb[:hi, cols], NT)
                delta = jnp.sum(wide * dweights, axis=-1, keepdims=True)
                ds = (wide * (dweights - delta) * HEAD_DIM ** (-0.5)).astype(jnp.bfloat16)
                dq01 = dot(ds, kb[:hi, cols], NN)
                dqb[:, cols] = jnp.where(low, dq01[:rows_c], dq01[rows_c:]).astype(jnp.bfloat16)
                dkb[:hi, cols] += dot(ds, q01, TN)
                dvb[:hi, cols] += dot(weights, d01, TN)
            dn = dot(dqb[...], weight(0), NN)
            dn += dot(dkb[lo:hi].astype(jnp.bfloat16), weight(1), NN)
            dn += dot(dvb[lo:hi].astype(jnp.bfloat16), weight(2), NN)
            h = hid[lo:hi].astype(jnp.float32)
            r = lax.rsqrt(jnp.mean(h * h, axis=-1, keepdims=True) + epsilon)
            along = jnp.mean(dn * h, axis=-1, keepdims=True)
            dh = dn * r - h * (r * r * r * along)
            gout[lo:hi] = (g.astype(jnp.float32) + dh).astype(jnp.bfloat16)
            backward_copy(c).start()

    half = width // 2

    def grad_block(place):
        cols = pl.ds(pl.multiple_of(place * (width // RING), width // RING), width // RING)
        block = dot(gin[:, cols], mixb[...], TN).astype(jnp.bfloat16)
        dw[pl.ds(place, 1)] = block.reshape(1, RING, width // RING // RING, width)

    first = {
        False: functools.partial(scatter_copy, lambda p: dw.at[p, :, :, :half], landa, rsend.at[0], rrecv.at[0], False),
        True: functools.partial(scatter_copy, lambda p: dw.at[:, p, :, half:], landb, rsend.at[1], rrecv.at[1], True),
    }
    second = {
        True: functools.partial(scatter_copy, lambda p: parta.at[p], enda, rsend.at[2], rrecv.at[2], True),
        False: functools.partial(scatter_copy, lambda p: partb.at[p], endb, rsend.at[3], rrecv.at[3], False),
    }
    for k in ORDER:
        grad_block(lax.rem(y + k, RING))
        first[False](k).start()
    grad_block(y)
    for k in ORDER:
        first[True](k).start()

    for along_z, own, land, part in ((False, dw[y, :, :, :half], landa, parta), (True, dw[:, z, :, half:], landb, partb)):
        total = own.astype(jnp.float32)
        for k in ORDER:
            first[along_z](k).wait_recv()
            total += land[k - 1].astype(jnp.float32)
        part[...] = total.astype(jnp.bfloat16)
        for k in ORDER:
            second[not along_z](k).start()
    for along_z, part, mine, land, cols in (
        (True, parta, z, enda, slice(0, half)), (False, partb, y, endb, slice(half, width))
    ):
        total = part[mine].astype(jnp.float32)
        for k in ORDER:
            second[along_z](k).wait_recv()
            total += land[k - 1].astype(jnp.float32)
        o_ref[:, cols] = total

    for k in ORDER:
        for along_z in (False, True):
            first[along_z](k).wait_send()
            second[along_z](k).wait_send()
    gather_end(w_ref, gsend, grecv)
    for c in range(NC):
        @pl.when(s < SECTIONS - 1)
        def _():
            forward_copy(c).wait_send()

        @pl.when(s > 0)
        def _():
            backward_copy(c).wait_send()


def pipeline(context, cot, bias, attn, out):
    length, width = context.shape
    rows_c = length // NC
    own = out.shape[0]
    full = pltpu.VMEM((length, width), jnp.bfloat16)
    landing = pltpu.VMEM((RING - 1, RING, own, width // 2), jnp.bfloat16)
    part = pltpu.VMEM((RING, own, width // 2), jnp.bfloat16)
    end = pltpu.VMEM((RING - 1, own, width // 2), jnp.bfloat16)
    return pl.pallas_call(
        pipeline_kernel,
        name="pipeline",
        out_shape=jax.ShapeDtypeStruct((own, width), jnp.float32),
        in_specs=[pl.BlockSpec(memory_space=pltpu.VMEM)] * 5,
        out_specs=pl.BlockSpec(memory_space=pltpu.VMEM),
        scratch_shapes=[
            pltpu.VMEM((4, RING, RING, own, width), jnp.bfloat16),
            pltpu.VMEM((RING, RING, own, width), jnp.bfloat16),
            landing, landing, part, part, end, end,
            pltpu.SemaphoreType.DMA((2, 4, 2, RING // 2)),
            pltpu.SemaphoreType.DMA((2, 4, 2, RING // 2)),
            pltpu.SemaphoreType.DMA((4, RING - 1)),
            pltpu.SemaphoreType.DMA((4, RING - 1)),
        ] + [full] * 8 + [
            pltpu.VMEM((NC, PAIRS, 2 * rows_c, length), jnp.bfloat16),
            pltpu.VMEM((rows_c, width), jnp.bfloat16),
            pltpu.VMEM((rows_c, width), jnp.bfloat16),
            pltpu.VMEM((length, width), jnp.float32),
            pltpu.VMEM((length, width), jnp.float32),
        ] + [pltpu.SemaphoreType.DMA((NC,))] * 4,
        compiler_params=pltpu.CompilerParams(
            collective_id=1, has_side_effects=True, vmem_limit_bytes=48 << 20
        ),
    )(context, cot, bias, attn, out)


def local(hidden_in, cotangent, segments, attn_weights, out_weight):
    section_index = lax.axis_index("section")
    context = hidden_in[0]
    length = context.shape[0]
    positions = jnp.arange(length, dtype=jnp.int32)
    causal = positions[None, :] <= positions[:, None]
    same_segment = segments[0][:, None] == segments[0][None, :]
    allowed = causal & (same_segment | (section_index % 2 == 1))
    bias = jnp.where(allowed, 0.0, masked_score).astype(jnp.float32)
    return pipeline(context, cotangent[0], bias, attn_weights[0], out_weight[0])[None]


def solution(mesh):
    in_specs = (
        P("dp", None, None),
        P("dp", None, None),
        P("dp", None),
        P("section", None, "dp", None),
        P("section", "dp", None),
    )
    return jax.shard_map(
        local, mesh=mesh, in_specs=in_specs, out_specs=P("section", "dp", None), check_vma=False
    )
```

```python
import functools
import jax
import jax.numpy as jnp
from jax import lax
from jax.experimental import pallas as pl
from jax.experimental.pallas import tpu as pltpu
from jax.sharding import PartitionSpec as P

MESH = pl.DeviceIdType.MESH
HEADS = 16
HEAD_DIM = 64
PAIRS = HEADS // 2
PAIR = 2 * HEAD_DIM
NC = 2
SECTIONS = 8
RING = 8
epsilon = 1e-05
masked_score = -1e30

NT = (((1,), (1,)), ((), ()))
NN = (((1,), (0,)), ((), ()))
TN = (((0,), (0,)), ((), ()))


def dot(a, b, dims):
    return lax.dot_general(a, b, dims, preferred_element_type=jnp.float32)


def halves(block, low):
    zero = jnp.zeros_like(block)
    return jnp.concatenate([jnp.where(low, block, zero), jnp.where(low, zero, block)], axis=0)


def first_steps(kind, way):
    return RING // 2 if (way == 1) == (kind == 0) else RING // 2 - 1


def second_steps(a, way):
    return RING // 2 if (way == 1) == (a % 2 == 0) else RING // 2 - 1


def place():
    d = lax.axis_index("dp")
    return d // RING, lax.rem(d, RING)


def around(me, step):
    return lax.rem(me + step + 2 * RING, RING)


def block_copy(w_ref, kind, y, z, other, send, recv):
    ref = w_ref.at[2 * kind : 2 * kind + 2, y, z]
    return pltpu.make_async_remote_copy(
        src_ref=ref, dst_ref=ref, send_sem=send, recv_sem=recv, device_id={"dp": other}, device_id_type=MESH
    )


def first_copy(w_ref, sends, recvs, kind, way, step):
    y, z = place()
    sems = sends.at[kind, (1 - way) // 2, step - 1], recvs.at[kind, (1 - way) // 2, step - 1]
    if kind == 0:
        return block_copy(w_ref, kind, y, around(z, -way * (step - 1)), y * RING + around(z, way), *sems)
    return block_copy(w_ref, kind, around(y, -way * (step - 1)), z, around(y, way) * RING + z, *sems)


def second_copy(w_ref, sends, recvs, kind, a, way, step):
    y, z = place()
    sems = sends.at[kind, a + 4, (1 - way) // 2, step - 1], recvs.at[kind, a + 4, (1 - way) // 2, step - 1]
    if kind == 0:
        return block_copy(
            w_ref, kind, around(y, -way * (step - 1)), around(z, a), around(y, way) * RING + z, *sems
        )
    return block_copy(w_ref, kind, around(y, a), around(z, -way * (step - 1)), y * RING + around(z, way), *sems)


def offsets(kind):
    return [0, -1, 1, -2, 2, -3, 3, 4 if kind == 1 else -4]


WAYS = (1, -1)


def gather(w_ref, send1, recv1, send2, recv2, beside):
    first = functools.partial(first_copy, w_ref, send1, recv1)
    second = functools.partial(second_copy, w_ref, send2, recv2)
    for kind in range(2):
        for way in WAYS:
            first(kind, way, 1).start()
    for kind in range(2):
        for way in WAYS:
            second(kind, 0, way, 1).start()
    for wave in range(1, RING + 1):
        for kind in range(2):
            for way in WAYS:
                if wave <= first_steps(kind, way):
                    first(kind, way, wave).wait_recv()
                    if wave < first_steps(kind, way):
                        first(kind, way, wave + 1).start()
                    for onward in WAYS:
                        second(kind, -way * wave, onward, 1).start()
        for a_index in range(RING):
            for kind in range(2):
                a = offsets(kind)[a_index]
                step = wave - abs(a)
                for way in WAYS:
                    if 1 <= step <= second_steps(a, way):
                        second(kind, a, way, step).wait_recv()
                        if step < second_steps(a, way):
                            second(kind, a, way, step + 1).start()
        beside(wave)


def gather_end(w_ref, send1, recv1, send2, recv2):
    for kind in range(2):
        for way in WAYS:
            for step in range(1, first_steps(kind, way) + 1):
                first_copy(w_ref, send1, recv1, kind, way, step).wait_send()
            for a in offsets(kind):
                for step in range(1, second_steps(a, way) + 1):
                    second_copy(w_ref, send2, recv2, kind, a, way, step).wait_send()


ORDER = (4, 3, 5, 2, 6, 1, 7)


def spread_copy(src, dst, send, recv, along_z, k):
    y, z = place()
    there = around(z if along_z else y, k)
    other = y * RING + there if along_z else there * RING + z
    return pltpu.make_async_remote_copy(
        src_ref=src(there), dst_ref=dst, send_sem=send.at[k - 1], recv_sem=recv.at[k - 1],
        device_id={"dp": other}, device_id_type=MESH,
    )


def pipeline_kernel(
    x_ref, cot_ref, seg_ref, attn_ref, out_ref, o_ref,
    w_ref, bias_ref, swap, gswap, mixes, gs, parts, ends,
    gsend1, grecv1, gsend2, grecv2, msend, mrecv, csend, crecv, esend, erecv, lsem,
    hid, outb, gin, gout, qb, kb, vb, mixb, pb, dmb, dqb, dkb, dvb,
    fsend, frecv, bsend, brecv,
):
    s = lax.axis_index("section")
    y, z = place()
    length, width = x_ref.shape
    rows_c = length // NC
    half = width // 2
    slice_cols = width // RING
    barrier = pltpu.get_barrier_semaphore()
    for step in (1, SECTIONS - 1):
        other = lax.rem(s + step, SECTIONS)
        pl.semaphore_signal(barrier, inc=1, device_id={"section": other}, device_id_type=MESH)
    for step in range(1, RING):
        for other in (around(y, step) * RING + z, y * RING + around(z, step)):
            pl.semaphore_signal(barrier, inc=1, device_id={"dp": other}, device_id_type=MESH)
    shard = [pltpu.make_async_copy(attn_ref.at[j], w_ref.at[j, y, z], lsem.at[j]) for j in range(3)]
    shard.append(pltpu.make_async_copy(out_ref, w_ref.at[3, y, z], lsem.at[3]))
    for copy in shard:
        copy.start()
    in_copy = pltpu.make_async_copy(x_ref, hid, lsem.at[4])
    cot_copy = pltpu.make_async_copy(cot_ref, gin, lsem.at[4])

    @pl.when(s == 0)
    def _():
        in_copy.start()

    @pl.when(s == SECTIONS - 1)
    def _():
        cot_copy.start()

    for copy in shard:
        copy.wait()
    pl.semaphore_wait(barrier, 2 + 2 * (RING - 1))
    own = slice_cols // RING

    def mask():
        ids = lax.broadcasted_iota(jnp.int32, (32, length), 0)
        one_hot = jnp.where(ids == seg_ref[...], 1.0, 0.0).astype(jnp.bfloat16)
        same = dot(one_hot, one_hot, TN) > 0.5
        query = lax.broadcasted_iota(jnp.int32, (length, length), 0)
        key = lax.broadcasted_iota(jnp.int32, (length, length), 1)
        any_segment = lax.broadcast(lax.rem(s, 2), (length, length)) == 1
        allowed = (key <= query) & (same | any_segment)
        bias_ref[...] = jnp.where(allowed, 0.0, masked_score)
        dkb[...] = jnp.zeros_like(dkb)
        dvb[...] = jnp.zeros_like(dvb)

    def swap_rows(j):
        row = lax.broadcasted_iota(jnp.int32, (slice_cols, width), 0) + j * slice_cols
        col = lax.broadcasted_iota(jnp.int32, (slice_cols, width), 1)
        source = lax.rem(col, slice_cols) // own * slice_cols + col // slice_cols * own + lax.rem(col, own)
        swap[j * slice_cols : (j + 1) * slice_cols] = jnp.where(row == source, 1.0, 0.0).astype(jnp.bfloat16)

    def beside(wave):
        swap_rows(wave - 1)
        if wave == 4:
            mask()

    gather(w_ref, gsend1, grecv1, gsend2, grecv2, beside)

    @pl.when(s == 0)
    def _():
        in_copy.wait()

    @pl.when(s == SECTIONS - 1)
    def _():
        cot_copy.wait()

    weight = lambda j: w_ref[j].reshape(width, width)

    def forward_copy(c):
        rows = pl.ds(c * rows_c, rows_c)
        return pltpu.make_async_remote_copy(
            src_ref=outb.at[rows], dst_ref=hid.at[rows], send_sem=fsend.at[c], recv_sem=frecv.at[c],
            device_id={"section": jnp.minimum(s + 1, SECTIONS - 1)}, device_id_type=MESH,
        )

    def backward_copy(c):
        rows = pl.ds(c * rows_c, rows_c)
        return pltpu.make_async_remote_copy(
            src_ref=gout.at[rows], dst_ref=gin.at[rows], send_sem=bsend.at[c], recv_sem=brecv.at[c],
            device_id={"section": jnp.maximum(s - 1, 0)}, device_id_type=MESH,
        )

    low = lax.broadcasted_iota(jnp.int32, (rows_c, PAIR), 1) < HEAD_DIM

    for c in range(NC):
        lo, hi = c * rows_c, (c + 1) * rows_c

        @pl.when(s > 0)
        def _():
            forward_copy(c).wait_recv()

        h = hid[lo:hi].astype(jnp.float32)
        r = lax.rsqrt(jnp.mean(h * h, axis=-1, keepdims=True) + epsilon)
        normed = (h * r).astype(jnp.bfloat16)
        for j, buf in ((0, qb), (1, kb), (2, vb)):
            buf[lo:hi] = dot(normed, weight(j), NT).astype(jnp.bfloat16)
        bias = bias_ref[lo:hi, :hi]
        bias2 = jnp.concatenate([bias, bias], axis=0)
        for p in range(PAIRS):
            cols = slice(p * PAIR, (p + 1) * PAIR)
            q01 = halves(qb[lo:hi, cols], low)
            scores = dot(q01, kb[:hi, cols], NT) * HEAD_DIM ** (-0.5) + bias2
            top = jnp.max(scores, axis=-1, keepdims=True)
            e = jnp.exp(scores - top)
            weights = (e / jnp.sum(e, axis=-1, keepdims=True)).astype(jnp.bfloat16)
            pb[c, p, :, :hi] = weights
            o = dot(weights, vb[:hi, cols], NN)
            mixb[lo:hi, cols] = jnp.where(low, o[:rows_c], o[rows_c:]).astype(jnp.bfloat16)

        @pl.when(s < SECTIONS - 1)
        def _():
            added = hid[lo:hi].astype(jnp.float32) + dot(mixb[lo:hi], weight(3), NT)
            outb[lo:hi] = added.astype(jnp.bfloat16)
            forward_copy(c).start()

    def mix_copy(along_z, k):
        cols = pl.ds(half if along_z else 0, half)
        return spread_copy(
            lambda there: mixb.at[:, cols], mixes.at[int(along_z), k], msend.at[int(along_z)],
            mrecv.at[int(along_z)], along_z, k,
        )

    def grad_copy(c, along_z, k):
        rows = pl.ds(c * rows_c, rows_c)
        source = gswap if along_z else gin
        return spread_copy(
            lambda there: source.at[rows, pl.ds(pl.multiple_of(there * slice_cols, slice_cols), slice_cols)],
            gs.at[int(along_z), k, rows], csend.at[int(along_z), c], crecv.at[int(along_z), c], along_z, k,
        )

    def end_copy(along_z, k):
        return spread_copy(
            lambda there: parts.at[int(not along_z), there], ends.at[int(not along_z), k - 1],
            esend.at[int(not along_z)], erecv.at[int(not along_z)], along_z, k,
        )

    for k in ORDER:
        for along_z in (False, True):
            mix_copy(along_z, k).start()

    for c in reversed(range(NC)):
        lo, hi = c * rows_c, (c + 1) * rows_c

        @pl.when(s < SECTIONS - 1)
        def _():
            backward_copy(c).wait_recv()

        @pl.when(s > 0)
        def _():
            g = gin[lo:hi]
            dmb[...] = dot(g, weight(3), NN).astype(jnp.bfloat16)
            for p in range(PAIRS):
                cols = slice(p * PAIR, (p + 1) * PAIR)
                d01 = halves(dmb[:, cols], low)
                q01 = halves(qb[lo:hi, cols], low)
                weights = pb[c, p, :, :hi]
                wide = weights.astype(jnp.float32)
                dweights = dot(d01, vb[:hi, cols], NT)
                delta = jnp.sum(wide * dweights, axis=-1, keepdims=True)
                ds = (wide * (dweights - delta) * HEAD_DIM ** (-0.5)).astype(jnp.bfloat16)
                dq01 = dot(ds, kb[:hi, cols], NN)
                dqb[:, cols] = jnp.where(low, dq01[:rows_c], dq01[rows_c:]).astype(jnp.bfloat16)
                dkb[:hi, cols] += dot(ds, q01, TN)
                dvb[:hi, cols] += dot(weights, d01, TN)
            dn = dot(dqb[...], weight(0), NN)
            dn += dot(dkb[lo:hi].astype(jnp.bfloat16), weight(1), NN)
            dn += dot(dvb[lo:hi].astype(jnp.bfloat16), weight(2), NN)
            h = hid[lo:hi].astype(jnp.float32)
            r = lax.rsqrt(jnp.mean(h * h, axis=-1, keepdims=True) + epsilon)
            along = jnp.mean(dn * h, axis=-1, keepdims=True)
            dh = dn * r - h * (r * r * r * along)
            gout[lo:hi] = (g.astype(jnp.float32) + dh).astype(jnp.bfloat16)
            backward_copy(c).start()

        for k in ORDER:
            grad_copy(c, False, k).start()
        gswap[lo:hi] = dot(gin[lo:hi], swap[...], NN).astype(jnp.bfloat16)
        for k in ORDER:
            grad_copy(c, True, k).start()

    for along_z in (False, True):
        i, me, source = int(along_z), (z if along_z else y), (gswap if along_z else gin)
        mixes[i, 0] = mixb[:, i * half : (i + 1) * half]
        gs[i, 0] = source[:, pl.ds(pl.multiple_of(me * slice_cols, slice_cols), slice_cols)]
        for k in ORDER:
            mix_copy(along_z, k).wait_recv()
            for c in range(NC):
                grad_copy(c, along_z, k).wait_recv()
        total = dot(
            gs[i].reshape(RING * length, slice_cols), mixes[i].reshape(RING * length, half), TN
        )
        parts[i] = total.astype(jnp.bfloat16).reshape(RING, own, half)
        for k in ORDER:
            end_copy(not along_z, k).start()
    for along_z in (False, True):
        i, me = int(along_z), (y if along_z else z)
        total = parts[i, me].astype(jnp.float32)
        for k in ORDER:
            end_copy(not along_z, k).wait_recv()
            total += ends[i, k - 1].astype(jnp.float32)
        o_ref[:, i * half : (i + 1) * half] = total

    for along_z in (False, True):
        for k in ORDER:
            mix_copy(along_z, k).wait_send()
            end_copy(along_z, k).wait_send()
            for c in range(NC):
                grad_copy(c, along_z, k).wait_send()
    gather_end(w_ref, gsend1, grecv1, gsend2, grecv2)
    for c in range(NC):
        @pl.when(s < SECTIONS - 1)
        def _():
            forward_copy(c).wait_send()

        @pl.when(s > 0)
        def _():
            backward_copy(c).wait_send()


def local(hidden_in, cotangent, segments, attn_weights, out_weight):
    length, width = hidden_in.shape[1:]
    own = out_weight.shape[1]
    rows_c = length // NC
    half = width // 2
    full = pltpu.VMEM((length, width), jnp.bfloat16)
    dma = lambda *shape: pltpu.SemaphoreType.DMA(shape)
    anywhere = pl.BlockSpec(memory_space=pl.ANY)
    result = pl.pallas_call(
        pipeline_kernel,
        name="pipeline",
        out_shape=jax.ShapeDtypeStruct((own, width), jnp.float32),
        in_specs=[anywhere, anywhere, pl.BlockSpec(memory_space=pltpu.VMEM), anywhere, anywhere],
        out_specs=pl.BlockSpec(memory_space=pltpu.VMEM),
        scratch_shapes=[
            pltpu.VMEM((4, RING, RING, own, width), jnp.bfloat16),
            pltpu.VMEM((length, length), jnp.float32),
            pltpu.VMEM((width, width), jnp.bfloat16),
            full,
            pltpu.VMEM((2, RING, length, half), jnp.bfloat16),
            pltpu.VMEM((2, RING, length, width // RING), jnp.bfloat16),
            pltpu.VMEM((2, RING, own, half), jnp.bfloat16),
            pltpu.VMEM((2, RING - 1, own, half), jnp.bfloat16),
            dma(2, 2, 4), dma(2, 2, 4), dma(2, 9, 2, 4), dma(2, 9, 2, 4),
            dma(2, RING - 1), dma(2, RING - 1), dma(2, NC, RING - 1), dma(2, NC, RING - 1),
            dma(2, RING - 1), dma(2, RING - 1), dma(5),
        ] + [full] * 8 + [
            pltpu.VMEM((NC, PAIRS, 2 * rows_c, length), jnp.bfloat16),
            pltpu.VMEM((rows_c, width), jnp.bfloat16),
            pltpu.VMEM((rows_c, width), jnp.bfloat16),
            pltpu.VMEM((length, width), jnp.float32),
            pltpu.VMEM((length, width), jnp.float32),
        ] + [dma(NC)] * 4,
        compiler_params=pltpu.CompilerParams(
            collective_id=1, has_side_effects=True, vmem_limit_bytes=56 << 20
        ),
    )(hidden_in[0], cotangent[0], segments, attn_weights[0], out_weight[0])
    return result[None]


def solution(mesh):
    in_specs = (
        P("dp", None, None),
        P("dp", None, None),
        P("dp", None),
        P("section", None, "dp", None),
        P("section", "dp", None),
    )
    return jax.shard_map(
        local, mesh=mesh, in_specs=in_specs, out_specs=P("section", "dp", None), check_vma=False
    )
```

```python
import functools
import jax
import jax.numpy as jnp
from jax import lax
from jax.experimental import pallas as pl
from jax.experimental.pallas import tpu as pltpu
from jax.sharding import PartitionSpec as P

MESH = pl.DeviceIdType.MESH
HEADS = 16
HEAD_DIM = 64
PAIRS = HEADS // 2
PAIR = 2 * HEAD_DIM
WIDE = 128
NC = 2
SECTIONS = 8
RING = 8
epsilon = 1e-05
masked_score = -1e30

NT = (((1,), (1,)), ((), ()))
NN = (((1,), (0,)), ((), ()))
TN = (((0,), (0,)), ((), ()))


def dot(a, b, dims):
    return lax.dot_general(a, b, dims, preferred_element_type=jnp.float32)


def halves(block, low):
    zero = jnp.zeros_like(block)
    return jnp.concatenate([jnp.where(low, block, zero), jnp.where(low, zero, block)], axis=0)


def first_steps(kind, way):
    return RING // 2 if (way == 1) == (kind == 0) else RING // 2 - 1


def second_steps(a, way):
    return RING // 2 if (way == 1) == (a % 2 == 0) else RING // 2 - 1


def place():
    d = lax.axis_index("dp")
    return d // RING, lax.rem(d, RING)


def around(me, step):
    return lax.rem(me + step + 2 * RING, RING)


def block_copy(w_ref, kind, y, z, other, send, recv):
    ref = w_ref.at[2 * kind : 2 * kind + 2, y, z]
    return pltpu.make_async_remote_copy(
        src_ref=ref, dst_ref=ref, send_sem=send, recv_sem=recv, device_id={"dp": other}, device_id_type=MESH
    )


def first_copy(w_ref, sends, recvs, kind, way, step):
    y, z = place()
    sems = sends.at[kind, (1 - way) // 2, step - 1], recvs.at[kind, (1 - way) // 2, step - 1]
    if kind == 0:
        return block_copy(w_ref, kind, y, around(z, -way * (step - 1)), y * RING + around(z, way), *sems)
    return block_copy(w_ref, kind, around(y, -way * (step - 1)), z, around(y, way) * RING + z, *sems)


def second_copy(w_ref, sends, recvs, kind, a, way, step):
    y, z = place()
    sems = sends.at[kind, a + 4, (1 - way) // 2, step - 1], recvs.at[kind, a + 4, (1 - way) // 2, step - 1]
    if kind == 0:
        return block_copy(
            w_ref, kind, around(y, -way * (step - 1)), around(z, a), around(y, way) * RING + z, *sems
        )
    return block_copy(w_ref, kind, around(y, a), around(z, -way * (step - 1)), y * RING + around(z, way), *sems)


def offsets(kind):
    return [0, -1, 1, -2, 2, -3, 3, 4 if kind == 1 else -4]


WAYS = (1, -1)


def gather(w_ref, send1, recv1, send2, recv2, beside):
    first = functools.partial(first_copy, w_ref, send1, recv1)
    second = functools.partial(second_copy, w_ref, send2, recv2)
    for kind in range(2):
        for way in WAYS:
            first(kind, way, 1).start()
    for kind in range(2):
        for way in WAYS:
            second(kind, 0, way, 1).start()
    for wave in range(1, RING + 1):
        for kind in range(2):
            for way in WAYS:
                if wave <= first_steps(kind, way):
                    first(kind, way, wave).wait_recv()
                    if wave < first_steps(kind, way):
                        first(kind, way, wave + 1).start()
                    for onward in WAYS:
                        second(kind, -way * wave, onward, 1).start()
        for a_index in reversed(range(RING)):
            for kind in range(2):
                a = offsets(kind)[a_index]
                step = wave - abs(a)
                for way in WAYS:
                    if 1 <= step <= second_steps(a, way):
                        second(kind, a, way, step).wait_recv()
                        if step < second_steps(a, way):
                            second(kind, a, way, step + 1).start()
        beside(wave)


def gather_end(w_ref, send1, recv1, send2, recv2):
    for kind in range(2):
        for way in WAYS:
            for step in range(1, first_steps(kind, way) + 1):
                first_copy(w_ref, send1, recv1, kind, way, step).wait_send()
            for a in offsets(kind):
                for step in range(1, second_steps(a, way) + 1):
                    second_copy(w_ref, send2, recv2, kind, a, way, step).wait_send()


ORDER = (4, 3, 5, 2, 6, 1, 7)


def spread_copy(src, dst, send, recv, along_z, k):
    y, z = place()
    there = around(z if along_z else y, k)
    other = y * RING + there if along_z else there * RING + z
    return pltpu.make_async_remote_copy(
        src_ref=src(there), dst_ref=dst, send_sem=send.at[k - 1], recv_sem=recv.at[k - 1],
        device_id={"dp": other}, device_id_type=MESH,
    )


def wide_halves(block, low):
    zero = jnp.zeros_like(block)
    gap = jnp.zeros((WIDE - block.shape[0], block.shape[1]), block.dtype)
    return jnp.concatenate([jnp.where(low, block, zero), gap, jnp.where(low, zero, block), gap], axis=0)


def pipeline_kernel(
    x_ref, cot_ref, seg_ref, attn_ref, out_ref, o_ref,
    w_ref, bias_ref, swap, gswap, mixes, gs, parts, ends,
    gsend1, grecv1, gsend2, grecv2, msend, mrecv, csend, crecv, esend, erecv, lsem,
    hid, outb, gin, gout, qb, kb, vb, mixb, pb, ptb, ktb, dsb, wtb, dmb, dqb, dkb, dvb,
    fsend, frecv, bsend, brecv,
):
    s = lax.axis_index("section")
    y, z = place()
    length, width = x_ref.shape
    rows_c = length // NC
    half = width // 2
    slice_cols = width // RING
    barrier = pltpu.get_barrier_semaphore()
    for step in (1, SECTIONS - 1):
        other = lax.rem(s + step, SECTIONS)
        pl.semaphore_signal(barrier, inc=1, device_id={"section": other}, device_id_type=MESH)
    for step in range(1, RING):
        for other in (around(y, step) * RING + z, y * RING + around(z, step)):
            pl.semaphore_signal(barrier, inc=1, device_id={"dp": other}, device_id_type=MESH)
    shard = [pltpu.make_async_copy(attn_ref.at[j], w_ref.at[j, y, z], lsem.at[j]) for j in range(3)]
    shard.append(pltpu.make_async_copy(out_ref, w_ref.at[3, y, z], lsem.at[3]))
    for copy in shard:
        copy.start()
    in_copy = pltpu.make_async_copy(x_ref, hid, lsem.at[4])
    cot_copy = pltpu.make_async_copy(cot_ref, gin, lsem.at[4])

    @pl.when(s == 0)
    def _():
        in_copy.start()

    @pl.when(s == SECTIONS - 1)
    def _():
        cot_copy.start()

    for copy in shard:
        copy.wait()
    pl.semaphore_wait(barrier, 2 + 2 * (RING - 1))
    own = slice_cols // RING

    def mask():
        ids = lax.broadcasted_iota(jnp.int32, (32, length), 0)
        one_hot = jnp.where(ids == seg_ref[...], 1.0, 0.0).astype(jnp.bfloat16)
        same = dot(one_hot, one_hot, TN) > 0.5
        query = lax.broadcasted_iota(jnp.int32, (length, length), 0)
        key = lax.broadcasted_iota(jnp.int32, (length, length), 1)
        any_segment = lax.broadcast(lax.rem(s, 2), (length, length)) == 1
        allowed = (key <= query) & (same | any_segment)
        bias_ref[...] = jnp.where(allowed, 0.0, masked_score)
        pb[...] = jnp.zeros_like(pb)
        kb[length:] = jnp.zeros((kb.shape[0] - length, width), kb.dtype)

    def swap_rows(j):
        row = lax.broadcasted_iota(jnp.int32, (slice_cols, width), 0) + j * slice_cols
        col = lax.broadcasted_iota(jnp.int32, (slice_cols, width), 1)
        source = lax.rem(col, slice_cols) // own * slice_cols + col // slice_cols * own + lax.rem(col, own)
        swap[j * slice_cols : (j + 1) * slice_cols] = jnp.where(row == source, 1.0, 0.0).astype(jnp.bfloat16)

    def beside(wave):
        swap_rows(wave - 1)
        if wave == 4:
            mask()

    gather(w_ref, gsend1, grecv1, gsend2, grecv2, beside)

    @pl.when(s == 0)
    def _():
        in_copy.wait()

    @pl.when(s == SECTIONS - 1)
    def _():
        cot_copy.wait()

    weight = lambda j: w_ref[j].reshape(width, width)

    def forward_copy(c):
        rows = pl.ds(c * rows_c, rows_c)
        return pltpu.make_async_remote_copy(
            src_ref=outb.at[rows], dst_ref=hid.at[rows], send_sem=fsend.at[c], recv_sem=frecv.at[c],
            device_id={"section": jnp.minimum(s + 1, SECTIONS - 1)}, device_id_type=MESH,
        )

    def backward_copy(c):
        rows = pl.ds(c * rows_c, rows_c)
        return pltpu.make_async_remote_copy(
            src_ref=gout.at[rows], dst_ref=gin.at[rows], send_sem=bsend.at[c], recv_sem=brecv.at[c],
            device_id={"section": jnp.maximum(s - 1, 0)}, device_id_type=MESH,
        )

    low_rows = lax.broadcasted_iota(jnp.int32, (PAIR, WIDE), 0) < HEAD_DIM
    low = lax.broadcasted_iota(jnp.int32, (rows_c, PAIR), 1) < HEAD_DIM

    for j in range(4):
        for i in range(RING):
            block = w_ref[j, i].reshape(slice_cols, width)
            wtb[j, :, i * slice_cols : (i + 1) * slice_cols] = block.T

    @pl.when(s >= SECTIONS // 2)
    def _():
        gather_end(w_ref, gsend1, grecv1, gsend2, grecv2)

    for c in range(NC):
        lo, hi = c * rows_c, (c + 1) * rows_c

        @pl.when(s > 0)
        def _():
            forward_copy(c).wait_recv()

        h = hid[lo:hi].astype(jnp.float32)
        r = lax.rsqrt(jnp.mean(h * h, axis=-1, keepdims=True) + epsilon)
        normed = (h * r).astype(jnp.bfloat16)
        for j, buf in ((0, qb), (1, kb), (2, vb)):
            buf[lo:hi] = dot(normed, wtb[j], NN).astype(jnp.bfloat16)
        bias = bias_ref[lo:hi, :hi]
        bias2 = jnp.concatenate([bias, bias], axis=0)
        for p in range(PAIRS):
            cols = slice(p * PAIR, (p + 1) * PAIR)
            q01 = halves(qb[lo:hi, cols], low)
            scores = dot(q01, kb[:hi, cols], NT) * HEAD_DIM ** (-0.5) + bias2
            top = jnp.max(scores, axis=-1, keepdims=True)
            e = jnp.exp(scores - top)
            weights = (e / jnp.sum(e, axis=-1, keepdims=True)).astype(jnp.bfloat16)
            pb[c, p, :rows_c, :hi] = weights[:rows_c]
            pb[c, p, WIDE : WIDE + rows_c, :hi] = weights[rows_c:]
        for p in range(PAIRS):
            cols = slice(p * PAIR, (p + 1) * PAIR)
            o = dot(pb[c, p, :, :hi], vb[:hi, cols], NN)
            mixb[lo:hi, cols] = jnp.where(low, o[:rows_c], o[WIDE : WIDE + rows_c]).astype(jnp.bfloat16)

        @pl.when(s < SECTIONS - 1)
        def _():
            added = hid[lo:hi].astype(jnp.float32) + dot(mixb[lo:hi], wtb[3], NN)
            outb[lo:hi] = added.astype(jnp.bfloat16)
            forward_copy(c).start()

    def mix_copy(along_z, k):
        cols = pl.ds(half if along_z else 0, half)
        return spread_copy(
            lambda there: mixb.at[:, cols], mixes.at[int(along_z), k], msend.at[int(along_z)],
            mrecv.at[int(along_z)], along_z, k,
        )

    def grad_copy(rows, c, along_z, k):
        source = gswap if along_z else gin
        return spread_copy(
            lambda there: source.at[rows, pl.ds(pl.multiple_of(there * slice_cols, slice_cols), slice_cols)],
            gs.at[int(along_z), k, rows], csend.at[int(along_z), c], crecv.at[int(along_z), c], along_z, k,
        )

    def exchange(rows, c):
        for k in ORDER:
            grad_copy(rows, c, False, k).start()
        gswap[rows] = dot(gin[rows], swap[...], NN).astype(jnp.bfloat16)
        for k in ORDER:
            grad_copy(rows, c, True, k).start()

    def exchanged(along_z, act):
        @pl.when(s == 0)
        def _():
            for k in ORDER:
                for c in range(NC):
                    act(grad_copy(pl.ds(c * rows_c, rows_c), c, along_z, k))

        @pl.when(s > 0)
        def _():
            for k in ORDER:
                act(grad_copy(pl.ds(0, length), 0, along_z, k))

    def end_copy(along_z, k):
        return spread_copy(
            lambda there: parts.at[int(not along_z), there], ends.at[int(not along_z), k - 1],
            esend.at[int(not along_z)], erecv.at[int(not along_z)], along_z, k,
        )

    for k in ORDER:
        for along_z in (False, True):
            mix_copy(along_z, k).start()

    def mix_end():
        for k in ORDER:
            for along_z in (False, True):
                mix_copy(along_z, k).wait_send()

    @pl.when(s < SECTIONS // 2)
    def _():
        gather_end(w_ref, gsend1, grecv1, gsend2, grecv2)

    @pl.when(s < 2)
    def _():
        mix_end()

    for c in range(NC):
        for p in range(PAIRS):
            ptb[c, p] = pb[c, p].T
    for p in range(PAIRS):
        cols = slice(p * PAIR, (p + 1) * PAIR)
        ktb[cols] = kb[:, cols].T

    for c in reversed(range(NC)):
        lo, hi = c * rows_c, (c + 1) * rows_c

        @pl.when(s < SECTIONS - 1)
        def _():
            backward_copy(c).wait_recv()

        @pl.when(s > 0)
        def _():
            g = gin[lo:hi]
            dmb[...] = dot(g, weight(3), NN).astype(jnp.bfloat16)
            for p in range(PAIRS):
                cols = slice(p * PAIR, (p + 1) * PAIR)
                d01 = wide_halves(dmb[:, cols], low)
                turned = ptb[c, p, :hi]
                wide = turned.astype(jnp.float32)
                dweights = dot(vb[:hi, cols], d01, NT)
                delta = jnp.sum(wide * dweights, axis=0, keepdims=True)
                dsb[p, :hi] = (wide * (dweights - delta) * HEAD_DIM ** (-0.5)).astype(jnp.bfloat16)
                dvalues = dot(turned, d01, NN)
                dvb[:hi, cols] = dvalues if c == NC - 1 else dvb[:hi, cols] + dvalues
            for p in range(PAIRS):
                cols = slice(p * PAIR, (p + 1) * PAIR)
                dq01 = dot(ktb[cols, :hi], dsb[p, :hi], NN)
                dqb[cols] = jnp.where(low_rows, dq01[:, :WIDE], dq01[:, WIDE:]).astype(jnp.bfloat16)
                dkeys = dot(dsb[p, :hi], wide_halves(qb[lo:hi, cols], low), NN)
                dkb[:hi, cols] = dkeys if c == NC - 1 else dkb[:hi, cols] + dkeys
            dn = dot(dqb[...], weight(0), TN)[:rows_c]
            dn += dot(dkb[lo:hi].astype(jnp.bfloat16), weight(1), NN)
            dn += dot(dvb[lo:hi].astype(jnp.bfloat16), weight(2), NN)
            h = hid[lo:hi].astype(jnp.float32)
            r = lax.rsqrt(jnp.mean(h * h, axis=-1, keepdims=True) + epsilon)
            along = jnp.mean(dn * h, axis=-1, keepdims=True)
            dh = dn * r - h * (r * r * r * along)
            gout[lo:hi] = (g.astype(jnp.float32) + dh).astype(jnp.bfloat16)
            backward_copy(c).start()

        @pl.when(s == 0)
        def _():
            exchange(pl.ds(lo, rows_c), c)

    @pl.when(s > 0)
    def _():
        exchange(pl.ds(0, length), 0)

    for along_z in (False, True):
        i, me, source = int(along_z), (z if along_z else y), (gswap if along_z else gin)
        mixes[i, 0] = mixb[:, i * half : (i + 1) * half]
        gs[i, 0] = source[:, pl.ds(pl.multiple_of(me * slice_cols, slice_cols), slice_cols)]
        for k in ORDER:
            mix_copy(along_z, k).wait_recv()
        exchanged(along_z, lambda copy: copy.wait_recv())
        total = dot(
            gs[i].reshape(RING * length, slice_cols), mixes[i].reshape(RING * length, half), TN
        )
        parts[i] = total.astype(jnp.bfloat16).reshape(RING, own, half)
        for k in ORDER:
            end_copy(not along_z, k).start()
    for along_z in (False, True):
        exchanged(along_z, lambda copy: copy.wait_send())

    @pl.when(s >= 2)
    def _():
        mix_end()

    for along_z in (False, True):
        i, me = int(along_z), (y if along_z else z)
        total = parts[i, me].astype(jnp.float32)
        for k in ORDER:
            end_copy(not along_z, k).wait_recv()
            total += ends[i, k - 1].astype(jnp.float32)
        o_ref[:, i * half : (i + 1) * half] = total

    for along_z in (False, True):
        for k in ORDER:
            end_copy(along_z, k).wait_send()
    for c in range(NC):
        @pl.when(s < SECTIONS - 1)
        def _():
            forward_copy(c).wait_send()

        @pl.when(s > 0)
        def _():
            backward_copy(c).wait_send()


def local(hidden_in, cotangent, segments, attn_weights, out_weight):
    length, width = hidden_in.shape[1:]
    own = out_weight.shape[1]
    rows_c = length // NC
    half = width // 2
    full = pltpu.VMEM((length, width), jnp.bfloat16)
    dma = lambda *shape: pltpu.SemaphoreType.DMA(shape)
    anywhere = pl.BlockSpec(memory_space=pl.ANY)
    result = pl.pallas_call(
        pipeline_kernel,
        name="pipeline",
        out_shape=jax.ShapeDtypeStruct((own, width), jnp.float32),
        in_specs=[anywhere, anywhere, pl.BlockSpec(memory_space=pltpu.VMEM), anywhere, anywhere],
        out_specs=pl.BlockSpec(memory_space=pltpu.VMEM),
        scratch_shapes=[
            pltpu.VMEM((4, RING, RING, own, width), jnp.bfloat16),
            pltpu.VMEM((length, length), jnp.float32),
            pltpu.VMEM((width, width), jnp.bfloat16),
            full,
            pltpu.VMEM((2, RING, length, half), jnp.bfloat16),
            pltpu.VMEM((2, RING, length, width // RING), jnp.bfloat16),
            pltpu.VMEM((2, RING, own, half), jnp.bfloat16),
            pltpu.VMEM((2, RING - 1, own, half), jnp.bfloat16),
            dma(2, 2, 4), dma(2, 2, 4), dma(2, 9, 2, 4), dma(2, 9, 2, 4),
            dma(2, RING - 1), dma(2, RING - 1), dma(2, NC, RING - 1), dma(2, NC, RING - 1),
            dma(2, RING - 1), dma(2, RING - 1), dma(5),
        ] + [full] * 5 + [pltpu.VMEM((2 * WIDE, width), jnp.bfloat16), full, full] + [
            pltpu.VMEM((NC, PAIRS, 2 * WIDE, 2 * WIDE), jnp.bfloat16),
            pltpu.VMEM((NC, PAIRS, 2 * WIDE, 2 * WIDE), jnp.bfloat16),
            pltpu.VMEM((width, 2 * WIDE), jnp.bfloat16),
            pltpu.VMEM((PAIRS, length, 2 * WIDE), jnp.bfloat16),
            pltpu.VMEM((4, width, width), jnp.bfloat16),
            pltpu.VMEM((rows_c, width), jnp.bfloat16),
            pltpu.VMEM((width, WIDE), jnp.bfloat16),
            pltpu.VMEM((length, width), jnp.float32),
            pltpu.VMEM((length, width), jnp.float32),
        ] + [dma(NC)] * 4,
        compiler_params=pltpu.CompilerParams(
            collective_id=1, has_side_effects=True, vmem_limit_bytes=56 << 20
        ),
    )(hidden_in[0], cotangent[0], segments, attn_weights[0], out_weight[0])
    return result[None]


def solution(mesh):
    in_specs = (
        P("dp", None, None),
        P("dp", None, None),
        P("dp", None),
        P("section", None, "dp", None),
        P("section", "dp", None),
    )
    return jax.shard_map(
        local, mesh=mesh, in_specs=in_specs, out_specs=P("section", "dp", None), check_vma=False
    )
```

```python
import functools
import jax
import jax.numpy as jnp
from jax import lax
from jax.experimental import pallas as pl
from jax.experimental.pallas import tpu as pltpu
from jax.sharding import PartitionSpec as P

MESH = pl.DeviceIdType.MESH
HEADS = 16
HEAD_DIM = 64
PAIRS = HEADS // 2
PAIR = 2 * HEAD_DIM
WIDE = 128
NC = 2
SECTIONS = 8
RING = 8
epsilon = 1e-05
masked_score = -1e30

NT = (((1,), (1,)), ((), ()))
NN = (((1,), (0,)), ((), ()))
TN = (((0,), (0,)), ((), ()))


def dot(a, b, dims):
    return lax.dot_general(a, b, dims, preferred_element_type=jnp.float32)


def halves(block, low):
    zero = jnp.zeros_like(block)
    return jnp.concatenate([jnp.where(low, block, zero), jnp.where(low, zero, block)], axis=0)


def first_steps(kind, way):
    return RING // 2 if (way == 1) == (kind == 0) else RING // 2 - 1


def second_steps(a, way):
    return RING // 2 if (way == 1) == (a % 2 == 0) else RING // 2 - 1


def place():
    d = lax.axis_index("dp")
    return d // RING, lax.rem(d, RING)


def around(me, step):
    return lax.rem(me + step + 2 * RING, RING)


def block_copy(w_ref, kind, y, z, other, send, recv):
    ref = w_ref.at[2 * kind : 2 * kind + 2, y, z]
    return pltpu.make_async_remote_copy(
        src_ref=ref, dst_ref=ref, send_sem=send, recv_sem=recv, device_id={"dp": other}, device_id_type=MESH
    )


def first_copy(w_ref, sends, recvs, kind, way, step):
    y, z = place()
    sems = sends.at[kind, (1 - way) // 2, step - 1], recvs.at[kind, (1 - way) // 2, step - 1]
    if kind == 0:
        return block_copy(w_ref, kind, y, around(z, -way * (step - 1)), y * RING + around(z, way), *sems)
    return block_copy(w_ref, kind, around(y, -way * (step - 1)), z, around(y, way) * RING + z, *sems)


def second_copy(w_ref, sends, recvs, kind, a, way, step):
    y, z = place()
    sems = sends.at[kind, a + 4, (1 - way) // 2, step - 1], recvs.at[kind, a + 4, (1 - way) // 2, step - 1]
    if kind == 0:
        return block_copy(
            w_ref, kind, around(y, -way * (step - 1)), around(z, a), around(y, way) * RING + z, *sems
        )
    return block_copy(w_ref, kind, around(y, a), around(z, -way * (step - 1)), y * RING + around(z, way), *sems)


def offsets(kind):
    return [0, -1, 1, -2, 2, -3, 3, 4 if kind == 1 else -4]


WAYS = (1, -1)


LIMIT = 6
TURN = 2


def gather(w_ref, send1, recv1, send2, recv2, beside, give_turn):
    first = functools.partial(first_copy, w_ref, send1, recv1)
    second = functools.partial(second_copy, w_ref, send2, recv2)
    under_way = {(axis, way): [] for axis in range(2) for way in WAYS}

    def start(axis, way, copy):
        queue = under_way[axis, way]
        if len(queue) == LIMIT:
            queue.pop(0).wait_send()
        copy.start()
        queue.append(copy)

    for kind in range(2):
        for way in WAYS:
            start(kind, way, first(kind, way, 1))
    for kind in range(2):
        for way in WAYS:
            start(1 - kind, way, second(kind, 0, way, 1))
    for wave in range(1, RING + 1):
        for kind in range(2):
            for way in WAYS:
                if wave <= first_steps(kind, way):
                    first(kind, way, wave).wait_recv()
                    if wave < first_steps(kind, way):
                        start(kind, way, first(kind, way, wave + 1))
                    for onward in WAYS:
                        start(1 - kind, onward, second(kind, -way * wave, onward, 1))
        for a_index in FAR:
            for kind in range(2):
                a = offsets(kind)[a_index]
                step = wave - abs(a)
                for way in WAYS:
                    if 1 <= step <= second_steps(a, way):
                        second(kind, a, way, step).wait_recv()
                        if step < second_steps(a, way):
                            start(1 - kind, way, second(kind, a, way, step + 1))
        beside(wave)
        if wave == TURN:
            give_turn()
    return [copy for queue in under_way.values() for copy in queue]


FAR = tuple(reversed(range(RING)))


ORDER = (4, 3, 5, 2, 6, 1, 7)


def spread_copy(src, dst, send, recv, along_z, k):
    y, z = place()
    there = around(z if along_z else y, k)
    other = y * RING + there if along_z else there * RING + z
    return pltpu.make_async_remote_copy(
        src_ref=src(there), dst_ref=dst, send_sem=send.at[k - 1], recv_sem=recv.at[k - 1],
        device_id={"dp": other}, device_id_type=MESH,
    )


def wide_halves(block, low):
    zero = jnp.zeros_like(block)
    gap = jnp.zeros((WIDE - block.shape[0], block.shape[1]), block.dtype)
    return jnp.concatenate([jnp.where(low, block, zero), gap, jnp.where(low, zero, block), gap], axis=0)


def pipeline_kernel(
    x_ref, cot_ref, seg_ref, attn_ref, out_ref, o_ref,
    w_ref, bias_ref, swap, gswap, mixes, gs, parts, ends,
    gsend1, grecv1, gsend2, grecv2, msend, mrecv, csend, crecv, esend, erecv, lsem, turn,
    hid, outb, gin, gout, qb, kb, vb, mixb, pb, ptb, ktb, dsb, wtb, dmb, dqb, dkb, dvb,
    fsend, frecv, bsend, brecv,
):
    s = lax.axis_index("section")
    y, z = place()
    length, width = x_ref.shape
    rows_c = length // NC
    half = width // 2
    slice_cols = width // RING
    barrier = pltpu.get_barrier_semaphore()
    for step in (1, SECTIONS - 1):
        other = lax.rem(s + step, SECTIONS)
        pl.semaphore_signal(barrier, inc=1, device_id={"section": other}, device_id_type=MESH)
    for step in range(1, RING):
        for other in (around(y, step) * RING + z, y * RING + around(z, step)):
            pl.semaphore_signal(barrier, inc=1, device_id={"dp": other}, device_id_type=MESH)
    shard = [pltpu.make_async_copy(attn_ref.at[j], w_ref.at[j, y, z], lsem.at[j]) for j in range(3)]
    shard.append(pltpu.make_async_copy(out_ref, w_ref.at[3, y, z], lsem.at[3]))
    for copy in shard:
        copy.start()
    in_copy = pltpu.make_async_copy(x_ref, hid, lsem.at[4])
    cot_copy = pltpu.make_async_copy(cot_ref, gin, lsem.at[4])

    @pl.when(s == 0)
    def _():
        in_copy.start()

    @pl.when(s == SECTIONS - 1)
    def _():
        cot_copy.start()

    for copy in shard:
        copy.wait()
    pl.semaphore_wait(barrier, 2 + 2 * (RING - 1))
    own = slice_cols // RING

    def mask():
        ids = lax.broadcasted_iota(jnp.int32, (32, length), 0)
        one_hot = jnp.where(ids == seg_ref[...], 1.0, 0.0).astype(jnp.bfloat16)
        same = dot(one_hot, one_hot, TN) > 0.5
        query = lax.broadcasted_iota(jnp.int32, (length, length), 0)
        key = lax.broadcasted_iota(jnp.int32, (length, length), 1)
        any_segment = lax.broadcast(lax.rem(s, 2), (length, length)) == 1
        allowed = (key <= query) & (same | any_segment)
        bias_ref[...] = jnp.where(allowed, 0.0, masked_score)
        pb[...] = jnp.zeros_like(pb)
        kb[length:] = jnp.zeros((kb.shape[0] - length, width), kb.dtype)

    def swap_rows(j):
        row = lax.broadcasted_iota(jnp.int32, (slice_cols, width), 0) + j * slice_cols
        col = lax.broadcasted_iota(jnp.int32, (slice_cols, width), 1)
        source = lax.rem(col, slice_cols) // own * slice_cols + col // slice_cols * own + lax.rem(col, own)
        swap[j * slice_cols : (j + 1) * slice_cols] = jnp.where(row == source, 1.0, 0.0).astype(jnp.bfloat16)

    def beside(wave):
        swap_rows(wave - 1)
        if wave == 4:
            mask()

    lead = lax.rem(s, 2) == 0

    def give_turn():
        @pl.when(lead)
        def _():
            pl.semaphore_signal(turn, inc=1, device_id={"section": s + 1 - 2 * lax.rem(s, 2)}, device_id_type=MESH)

    @pl.when(jnp.logical_not(lead))
    def _():
        pl.semaphore_wait(turn, 1)

    unsent = gather(w_ref, gsend1, grecv1, gsend2, grecv2, beside, give_turn)

    @pl.when(s == 0)
    def _():
        in_copy.wait()

    @pl.when(s == SECTIONS - 1)
    def _():
        cot_copy.wait()

    weight = lambda j: w_ref[j].reshape(width, width)

    def forward_copy(c):
        rows = pl.ds(c * rows_c, rows_c)
        return pltpu.make_async_remote_copy(
            src_ref=outb.at[rows], dst_ref=hid.at[rows], send_sem=fsend.at[c], recv_sem=frecv.at[c],
            device_id={"section": jnp.minimum(s + 1, SECTIONS - 1)}, device_id_type=MESH,
        )

    def backward_copy(c):
        rows = pl.ds(c * rows_c, rows_c)
        return pltpu.make_async_remote_copy(
            src_ref=gout.at[rows], dst_ref=gin.at[rows], send_sem=bsend.at[c], recv_sem=brecv.at[c],
            device_id={"section": jnp.maximum(s - 1, 0)}, device_id_type=MESH,
        )

    low_rows = lax.broadcasted_iota(jnp.int32, (PAIR, WIDE), 0) < HEAD_DIM
    low = lax.broadcasted_iota(jnp.int32, (rows_c, PAIR), 1) < HEAD_DIM

    for j in range(4):
        for i in range(RING):
            block = w_ref[j, i].reshape(slice_cols, width)
            wtb[j, :, i * slice_cols : (i + 1) * slice_cols] = block.T

    for c in range(NC):
        lo, hi = c * rows_c, (c + 1) * rows_c

        @pl.when(s > 0)
        def _():
            forward_copy(c).wait_recv()

        h = hid[lo:hi].astype(jnp.float32)
        r = lax.rsqrt(jnp.mean(h * h, axis=-1, keepdims=True) + epsilon)
        normed = (h * r).astype(jnp.bfloat16)
        qb[lo:hi] = (dot(normed, wtb[0], NN) * HEAD_DIM ** (-0.5)).astype(jnp.bfloat16)
        kb[lo:hi] = dot(normed, wtb[1], NN).astype(jnp.bfloat16)
        bias = bias_ref[lo:hi, :hi]
        bias2 = jnp.concatenate([bias, bias], axis=0)
        for p in range(PAIRS):
            cols = slice(p * PAIR, (p + 1) * PAIR)
            q01 = halves(qb[lo:hi, cols], low)
            scores = dot(q01, kb[:hi, cols], NT) + bias2
            top = jnp.max(scores, axis=-1, keepdims=True)
            e = jnp.exp(scores - top)
            weights = (e * (1.0 / jnp.sum(e, axis=-1, keepdims=True))).astype(jnp.bfloat16)
            pb[c, p, :rows_c, :hi] = weights[:rows_c]
            pb[c, p, WIDE : WIDE + rows_c, :hi] = weights[rows_c:]
            if p % 2 == 0:
                two = slice(p * PAIR, (p + 2) * PAIR)
                vb[lo:hi, two] = dot(normed, wtb[2, :, two], NN).astype(jnp.bfloat16)
        for p in range(PAIRS):
            cols = slice(p * PAIR, (p + 1) * PAIR)
            o = dot(pb[c, p, :, :hi], vb[:hi, cols], NN)
            mixb[lo:hi, cols] = jnp.where(low, o[:rows_c], o[WIDE : WIDE + rows_c]).astype(jnp.bfloat16)

        @pl.when(s < SECTIONS - 1)
        def _():
            added = hid[lo:hi].astype(jnp.float32) + dot(mixb[lo:hi], wtb[3], NN)
            outb[lo:hi] = added.astype(jnp.bfloat16)
            forward_copy(c).start()

    def mix_copy(along_z, k):
        cols = pl.ds(half if along_z else 0, half)
        return spread_copy(
            lambda there: mixb.at[:, cols], mixes.at[int(along_z), k], msend.at[int(along_z)],
            mrecv.at[int(along_z)], along_z, k,
        )

    def grad_copy(rows, c, along_z, k):
        source = gswap if along_z else gin
        return spread_copy(
            lambda there: source.at[rows, pl.ds(pl.multiple_of(there * slice_cols, slice_cols), slice_cols)],
            gs.at[int(along_z), k, rows], csend.at[int(along_z), c], crecv.at[int(along_z), c], along_z, k,
        )

    def exchange(rows, c):
        for k in ORDER:
            grad_copy(rows, c, False, k).start()
        gswap[rows] = dot(gin[rows], swap[...], NN).astype(jnp.bfloat16)
        for k in ORDER:
            grad_copy(rows, c, True, k).start()

    def exchanged(along_z, act):
        @pl.when(s == 0)
        def _():
            for k in ORDER:
                for c in range(NC):
                    act(grad_copy(pl.ds(c * rows_c, rows_c), c, along_z, k))

        @pl.when(s > 0)
        def _():
            for k in ORDER:
                act(grad_copy(pl.ds(0, length), 0, along_z, k))

    def end_copy(along_z, k):
        return spread_copy(
            lambda there: parts.at[int(not along_z), there], ends.at[int(not along_z), k - 1],
            esend.at[int(not along_z)], erecv.at[int(not along_z)], along_z, k,
        )

    for k in ORDER:
        for along_z in (False, True):
            mix_copy(along_z, k).start()

    def mix_end():
        for k in ORDER:
            for along_z in (False, True):
                mix_copy(along_z, k).wait_send()

    for copy in unsent:
        copy.wait_send()

    @pl.when(s < 2)
    def _():
        mix_end()

    for c in range(NC):
        for p in range(PAIRS):
            ptb[c, p] = pb[c, p].T
    for p in range(PAIRS):
        cols = slice(p * PAIR, (p + 1) * PAIR)
        ktb[cols] = (kb[:, cols] * HEAD_DIM ** (-0.5)).T

    for c in reversed(range(NC)):
        lo, hi = c * rows_c, (c + 1) * rows_c

        @pl.when(s < SECTIONS - 1)
        def _():
            backward_copy(c).wait_recv()

        @pl.when(s > 0)
        def _():
            g = gin[lo:hi]
            dmb[...] = dot(g, weight(3), NN).astype(jnp.bfloat16)
            for p in range(PAIRS):
                cols = slice(p * PAIR, (p + 1) * PAIR)
                d01 = wide_halves(dmb[:, cols], low)
                turned = ptb[c, p, :hi]
                wide = turned.astype(jnp.float32)
                dweights = dot(vb[:hi, cols], d01, NT)
                delta = jnp.sum(wide * dweights, axis=0, keepdims=True)
                dsb[p, :hi] = (wide * (dweights - delta)).astype(jnp.bfloat16)
                dvalues = dot(turned, d01, NN)
                dvb[:hi, cols] = dvalues if c == NC - 1 else dvb[:hi, cols] + dvalues
            for p in range(PAIRS):
                cols = slice(p * PAIR, (p + 1) * PAIR)
                dq01 = dot(ktb[cols, :hi], dsb[p, :hi], NN)
                dqb[cols] = jnp.where(low_rows, dq01[:, :WIDE], dq01[:, WIDE:]).astype(jnp.bfloat16)
                dkeys = dot(dsb[p, :hi], wide_halves(qb[lo:hi, cols], low), NN)
                dkb[:hi, cols] = dkeys if c == NC - 1 else dkb[:hi, cols] + dkeys
            dn = dot(dqb[...], weight(0), TN)[:rows_c]
            dn += dot(dkb[lo:hi].astype(jnp.bfloat16), weight(1), NN)
            dn += dot(dvb[lo:hi].astype(jnp.bfloat16), weight(2), NN)
            h = hid[lo:hi].astype(jnp.float32)
            r = lax.rsqrt(jnp.mean(h * h, axis=-1, keepdims=True) + epsilon)
            along = jnp.mean(dn * h, axis=-1, keepdims=True)
            dh = dn * r - h * (r * r * r * along)
            gout[lo:hi] = (g.astype(jnp.float32) + dh).astype(jnp.bfloat16)
            backward_copy(c).start()

        @pl.when(s == 0)
        def _():
            exchange(pl.ds(lo, rows_c), c)

    @pl.when(s > 0)
    def _():
        exchange(pl.ds(0, length), 0)

    for along_z in (False, True):
        i, me, source = int(along_z), (z if along_z else y), (gswap if along_z else gin)
        mixes[i, 0] = mixb[:, i * half : (i + 1) * half]
        gs[i, 0] = source[:, pl.ds(pl.multiple_of(me * slice_cols, slice_cols), slice_cols)]
        for k in ORDER:
            mix_copy(along_z, k).wait_recv()
        exchanged(along_z, lambda copy: copy.wait_recv())
        total = dot(
            gs[i].reshape(RING * length, slice_cols), mixes[i].reshape(RING * length, half), TN
        )
        parts[i] = total.astype(jnp.bfloat16).reshape(RING, own, half)
        for k in ORDER:
            end_copy(not along_z, k).start()
    for along_z in (False, True):
        exchanged(along_z, lambda copy: copy.wait_send())

    @pl.when(s >= 2)
    def _():
        mix_end()

    for along_z in (False, True):
        i, me = int(along_z), (y if along_z else z)
        total = parts[i, me].astype(jnp.float32)
        for k in ORDER:
            end_copy(not along_z, k).wait_recv()
            total += ends[i, k - 1].astype(jnp.float32)
        o_ref[:, i * half : (i + 1) * half] = total

    for along_z in (False, True):
        for k in ORDER:
            end_copy(along_z, k).wait_send()
    for c in range(NC):
        @pl.when(s < SECTIONS - 1)
        def _():
            forward_copy(c).wait_send()

        @pl.when(s > 0)
        def _():
            backward_copy(c).wait_send()


def local(hidden_in, cotangent, segments, attn_weights, out_weight):
    length, width = hidden_in.shape[1:]
    own = out_weight.shape[1]
    rows_c = length // NC
    half = width // 2
    full = pltpu.VMEM((length, width), jnp.bfloat16)
    dma = lambda *shape: pltpu.SemaphoreType.DMA(shape)
    anywhere = pl.BlockSpec(memory_space=pl.ANY)
    result = pl.pallas_call(
        pipeline_kernel,
        name="pipeline",
        out_shape=jax.ShapeDtypeStruct((own, width), jnp.float32),
        in_specs=[anywhere, anywhere, pl.BlockSpec(memory_space=pltpu.VMEM), anywhere, anywhere],
        out_specs=pl.BlockSpec(memory_space=pltpu.VMEM),
        scratch_shapes=[
            pltpu.VMEM((4, RING, RING, own, width), jnp.bfloat16),
            pltpu.VMEM((length, length), jnp.float32),
            pltpu.VMEM((width, width), jnp.bfloat16),
            full,
            pltpu.VMEM((2, RING, length, half), jnp.bfloat16),
            pltpu.VMEM((2, RING, length, width // RING), jnp.bfloat16),
            pltpu.VMEM((2, RING, own, half), jnp.bfloat16),
            pltpu.VMEM((2, RING - 1, own, half), jnp.bfloat16),
            dma(2, 2, 4), dma(2, 2, 4), dma(2, 9, 2, 4), dma(2, 9, 2, 4),
            dma(2, RING - 1), dma(2, RING - 1), dma(2, NC, RING - 1), dma(2, NC, RING - 1),
            dma(2, RING - 1), dma(2, RING - 1), dma(5), pltpu.SemaphoreType.REGULAR,
        ] + [full] * 5 + [pltpu.VMEM((2 * WIDE, width), jnp.bfloat16), full, full] + [
            pltpu.VMEM((NC, PAIRS, 2 * WIDE, 2 * WIDE), jnp.bfloat16),
            pltpu.VMEM((NC, PAIRS, 2 * WIDE, 2 * WIDE), jnp.bfloat16),
            pltpu.VMEM((width, 2 * WIDE), jnp.bfloat16),
            pltpu.VMEM((PAIRS, length, 2 * WIDE), jnp.bfloat16),
            pltpu.VMEM((4, width, width), jnp.bfloat16),
            pltpu.VMEM((rows_c, width), jnp.bfloat16),
            pltpu.VMEM((width, WIDE), jnp.bfloat16),
            pltpu.VMEM((length, width), jnp.float32),
            pltpu.VMEM((length, width), jnp.float32),
        ] + [dma(NC)] * 4,
        compiler_params=pltpu.CompilerParams(
            collective_id=1, has_side_effects=True, vmem_limit_bytes=56 << 20
        ),
    )(hidden_in[0], cotangent[0], segments, attn_weights[0], out_weight[0])
    return result[None]


def solution(mesh):
    in_specs = (
        P("dp", None, None),
        P("dp", None, None),
        P("dp", None),
        P("section", None, "dp", None),
        P("section", "dp", None),
    )
    return jax.shard_map(
        local, mesh=mesh, in_specs=in_specs, out_specs=P("section", "dp", None), check_vma=False
    )
```

```python
import functools
import jax
import jax.numpy as jnp
from jax import lax
from jax.experimental import pallas as pl
from jax.experimental.pallas import tpu as pltpu
from jax.sharding import PartitionSpec as P

MESH = pl.DeviceIdType.MESH
HEADS = 16
HEAD_DIM = 64
PAIRS = HEADS // 2
PAIR = 2 * HEAD_DIM
WIDE = 128
NC = 2
BY_CHUNK = 2
SECTIONS = 8
RING = 8
epsilon = 1e-05
masked_score = -1e30

NT = (((1,), (1,)), ((), ()))
NN = (((1,), (0,)), ((), ()))
TN = (((0,), (0,)), ((), ()))


def dot(a, b, dims):
    return lax.dot_general(a, b, dims, preferred_element_type=jnp.float32)


def halves(block, low):
    zero = jnp.zeros_like(block)
    return jnp.concatenate([jnp.where(low, block, zero), jnp.where(low, zero, block)], axis=0)


def first_steps(kind, way):
    return RING // 2 if (way == 1) == (kind == 0) else RING // 2 - 1


def second_steps(a, way):
    return RING // 2 if (way == 1) == (a % 2 == 0) else RING // 2 - 1


def place():
    d = lax.axis_index("dp")
    return d // RING, lax.rem(d, RING)


def around(me, step):
    return lax.rem(me + step + 2 * RING, RING)


def block_copy(w_ref, kind, y, z, other, send, recv):
    ref = w_ref.at[2 * kind : 2 * kind + 2, y, z]
    return pltpu.make_async_remote_copy(
        src_ref=ref, dst_ref=ref, send_sem=send, recv_sem=recv, device_id={"dp": other}, device_id_type=MESH
    )


def first_copy(w_ref, sends, recvs, kind, way, step):
    y, z = place()
    sems = sends.at[kind, (1 - way) // 2, step - 1], recvs.at[kind, (1 - way) // 2, step - 1]
    if kind == 0:
        return block_copy(w_ref, kind, y, around(z, -way * (step - 1)), y * RING + around(z, way), *sems)
    return block_copy(w_ref, kind, around(y, -way * (step - 1)), z, around(y, way) * RING + z, *sems)


def second_copy(w_ref, sends, recvs, kind, a, way, step):
    y, z = place()
    sems = sends.at[kind, a + 4, (1 - way) // 2, step - 1], recvs.at[kind, a + 4, (1 - way) // 2, step - 1]
    if kind == 0:
        return block_copy(
            w_ref, kind, around(y, -way * (step - 1)), around(z, a), around(y, way) * RING + z, *sems
        )
    return block_copy(w_ref, kind, around(y, a), around(z, -way * (step - 1)), y * RING + around(z, way), *sems)


def offsets(kind):
    return [0, -1, 1, -2, 2, -3, 3, 4 if kind == 1 else -4]


WAYS = (1, -1)


LIMIT = 6
TURN = 2


def gather(w_ref, send1, recv1, send2, recv2, beside, give_turn):
    first = functools.partial(first_copy, w_ref, send1, recv1)
    second = functools.partial(second_copy, w_ref, send2, recv2)
    under_way = {(axis, way): [] for axis in range(2) for way in WAYS}

    def start(axis, way, copy):
        queue = under_way[axis, way]
        if len(queue) == LIMIT:
            queue.pop(0).wait_send()
        copy.start()
        queue.append(copy)

    for kind in range(2):
        for way in WAYS:
            start(kind, way, first(kind, way, 1))
    for kind in range(2):
        for way in WAYS:
            start(1 - kind, way, second(kind, 0, way, 1))
    for wave in range(1, RING + 1):
        for kind in range(2):
            for way in WAYS:
                if wave <= first_steps(kind, way):
                    first(kind, way, wave).wait_recv()
                    if wave < first_steps(kind, way):
                        start(kind, way, first(kind, way, wave + 1))
                    for onward in WAYS:
                        start(1 - kind, onward, second(kind, -way * wave, onward, 1))
        for a_index in FAR:
            for kind in range(2):
                a = offsets(kind)[a_index]
                step = wave - abs(a)
                for way in WAYS:
                    if 1 <= step <= second_steps(a, way):
                        second(kind, a, way, step).wait_recv()
                        if step < second_steps(a, way):
                            start(1 - kind, way, second(kind, a, way, step + 1))
        beside(wave)
        if wave == TURN:
            give_turn()
    return [copy for queue in under_way.values() for copy in queue]


FAR = tuple(reversed(range(RING)))


ORDER = (4, 3, 5, 2, 6, 1, 7)


def spread_copy(src, dst, send, recv, along_z, k):
    y, z = place()
    there = around(z if along_z else y, k)
    other = y * RING + there if along_z else there * RING + z
    return pltpu.make_async_remote_copy(
        src_ref=src(there), dst_ref=dst, send_sem=send.at[k - 1], recv_sem=recv.at[k - 1],
        device_id={"dp": other}, device_id_type=MESH,
    )


def wide_halves(block, low):
    zero = jnp.zeros_like(block)
    gap = jnp.zeros((WIDE - block.shape[0], block.shape[1]), block.dtype)
    return jnp.concatenate([jnp.where(low, block, zero), gap, jnp.where(low, zero, block), gap], axis=0)


def pipeline_kernel(
    x_ref, cot_ref, seg_ref, attn_ref, out_ref, o_ref,
    w_ref, bias_ref, swap, gswap, mixes, gs, parts, ends,
    gsend1, grecv1, gsend2, grecv2, msend, mrecv, csend, crecv, esend, erecv, lsem, turn,
    hid, outb, gin, gout, qb, kb, vb, mixb, pb, ptb, ktb, dsb, wtb, dmb, dqb, dkb, dvb,
    fsend, frecv, bsend, brecv,
):
    s = lax.axis_index("section")
    y, z = place()
    length, width = x_ref.shape
    rows_c = length // NC
    half = width // 2
    slice_cols = width // RING
    barrier = pltpu.get_barrier_semaphore()
    for step in (1, SECTIONS - 1):
        other = lax.rem(s + step, SECTIONS)
        pl.semaphore_signal(barrier, inc=1, device_id={"section": other}, device_id_type=MESH)
    for step in range(1, RING):
        for other in (around(y, step) * RING + z, y * RING + around(z, step)):
            pl.semaphore_signal(barrier, inc=1, device_id={"dp": other}, device_id_type=MESH)
    shard = [pltpu.make_async_copy(attn_ref.at[j], w_ref.at[j, y, z], lsem.at[j]) for j in range(3)]
    shard.append(pltpu.make_async_copy(out_ref, w_ref.at[3, y, z], lsem.at[3]))
    for copy in shard:
        copy.start()
    in_copy = pltpu.make_async_copy(x_ref, hid, lsem.at[4])
    cot_copy = pltpu.make_async_copy(cot_ref, gin, lsem.at[4])

    @pl.when(s == 0)
    def _():
        in_copy.start()

    @pl.when(s == SECTIONS - 1)
    def _():
        cot_copy.start()

    for copy in shard:
        copy.wait()
    pl.semaphore_wait(barrier, 2 + 2 * (RING - 1))
    own = slice_cols // RING

    def mask():
        ids = lax.broadcasted_iota(jnp.int32, (32, length), 0)
        one_hot = jnp.where(ids == seg_ref[...], 1.0, 0.0).astype(jnp.bfloat16)
        same = dot(one_hot, one_hot, TN) > 0.5
        query = lax.broadcasted_iota(jnp.int32, (length, length), 0)
        key = lax.broadcasted_iota(jnp.int32, (length, length), 1)
        any_segment = lax.broadcast(lax.rem(s, 2), (length, length)) == 1
        allowed = (key <= query) & (same | any_segment)
        bias_ref[...] = jnp.where(allowed, 0.0, masked_score)
        pb[...] = jnp.zeros_like(pb)
        kb[length:] = jnp.zeros((kb.shape[0] - length, width), kb.dtype)

    def swap_rows(j):
        row = lax.broadcasted_iota(jnp.int32, (slice_cols, width), 0) + j * slice_cols
        col = lax.broadcasted_iota(jnp.int32, (slice_cols, width), 1)
        source = lax.rem(col, slice_cols) // own * slice_cols + col // slice_cols * own + lax.rem(col, own)
        swap[j * slice_cols : (j + 1) * slice_cols] = jnp.where(row == source, 1.0, 0.0).astype(jnp.bfloat16)

    def beside(wave):
        swap_rows(wave - 1)
        if wave == 4:
            mask()

    lead = lax.rem(s, 2) == 0

    def give_turn():
        @pl.when(lead)
        def _():
            pl.semaphore_signal(turn, inc=1, device_id={"section": s + 1 - 2 * lax.rem(s, 2)}, device_id_type=MESH)

    @pl.when(jnp.logical_not(lead))
    def _():
        pl.semaphore_wait(turn, 1)

    unsent = gather(w_ref, gsend1, grecv1, gsend2, grecv2, beside, give_turn)

    @pl.when(s == 0)
    def _():
        in_copy.wait()

    @pl.when(s == SECTIONS - 1)
    def _():
        cot_copy.wait()

    weight = lambda j: w_ref[j].reshape(width, width)

    def forward_copy(c):
        rows = pl.ds(c * rows_c, rows_c)
        return pltpu.make_async_remote_copy(
            src_ref=outb.at[rows], dst_ref=hid.at[rows], send_sem=fsend.at[c], recv_sem=frecv.at[c],
            device_id={"section": jnp.minimum(s + 1, SECTIONS - 1)}, device_id_type=MESH,
        )

    def backward_copy(c):
        rows = pl.ds(c * rows_c, rows_c)
        return pltpu.make_async_remote_copy(
            src_ref=gout.at[rows], dst_ref=gin.at[rows], send_sem=bsend.at[c], recv_sem=brecv.at[c],
            device_id={"section": jnp.maximum(s - 1, 0)}, device_id_type=MESH,
        )

    def turn_weights(c):
        for p in range(PAIRS):
            ptb[c, p] = pb[c, p].T

    low_rows = lax.broadcasted_iota(jnp.int32, (PAIR, WIDE), 0) < HEAD_DIM
    low = lax.broadcasted_iota(jnp.int32, (rows_c, PAIR), 1) < HEAD_DIM

    for j in range(4):
        for i in range(RING):
            block = w_ref[j, i].reshape(slice_cols, width)
            wtb[j, :, i * slice_cols : (i + 1) * slice_cols] = block.T

    for c in range(NC):
        lo, hi = c * rows_c, (c + 1) * rows_c

        @pl.when(s > 0)
        def _():
            forward_copy(c).wait_recv()

        h = hid[lo:hi].astype(jnp.float32)
        r = lax.rsqrt(jnp.mean(h * h, axis=-1, keepdims=True) + epsilon)
        normed = (h * r).astype(jnp.bfloat16)
        qb[lo:hi] = (dot(normed, wtb[0], NN) * HEAD_DIM ** (-0.5)).astype(jnp.bfloat16)
        kb[lo:hi] = dot(normed, wtb[1], NN).astype(jnp.bfloat16)
        bias = bias_ref[lo:hi, :hi]
        bias2 = jnp.concatenate([bias, bias], axis=0)
        for p in range(PAIRS):
            cols = slice(p * PAIR, (p + 1) * PAIR)
            q01 = halves(qb[lo:hi, cols], low)
            scores = dot(q01, kb[:hi, cols], NT) + bias2
            top = jnp.max(scores, axis=-1, keepdims=True)
            e = jnp.exp(scores - top)
            weights = (e * (1.0 / jnp.sum(e, axis=-1, keepdims=True))).astype(jnp.bfloat16)
            pb[c, p, :rows_c, :hi] = weights[:rows_c]
            pb[c, p, WIDE : WIDE + rows_c, :hi] = weights[rows_c:]
            if p % 2 == 0:
                two = slice(p * PAIR, (p + 2) * PAIR)
                vb[lo:hi, two] = dot(normed, wtb[2, :, two], NN).astype(jnp.bfloat16)
        for p in range(PAIRS):
            cols = slice(p * PAIR, (p + 1) * PAIR)
            o = dot(pb[c, p, :, :hi], vb[:hi, cols], NN)
            mixb[lo:hi, cols] = jnp.where(low, o[:rows_c], o[WIDE : WIDE + rows_c]).astype(jnp.bfloat16)

        @pl.when(s < SECTIONS - 1)
        def _():
            added = hid[lo:hi].astype(jnp.float32) + dot(mixb[lo:hi], wtb[3], NN)
            outb[lo:hi] = added.astype(jnp.bfloat16)
            forward_copy(c).start()

        if c == 0:
            @pl.when(s == SECTIONS - 1)
            def _():
                turn_weights(0)

    def mix_copy(along_z, k):
        cols = pl.ds(half if along_z else 0, half)
        return spread_copy(
            lambda there: mixb.at[:, cols], mixes.at[int(along_z), k], msend.at[int(along_z)],
            mrecv.at[int(along_z)], along_z, k,
        )

    def grad_copy(rows, c, along_z, k):
        source = gswap if along_z else gin
        return spread_copy(
            lambda there: source.at[rows, pl.ds(pl.multiple_of(there * slice_cols, slice_cols), slice_cols)],
            gs.at[int(along_z), k, rows], csend.at[int(along_z), c], crecv.at[int(along_z), c], along_z, k,
        )

    def exchange(rows, c):
        for k in ORDER:
            grad_copy(rows, c, False, k).start()
        gswap[rows] = dot(gin[rows], swap[...], NN).astype(jnp.bfloat16)
        for k in ORDER:
            grad_copy(rows, c, True, k).start()

    def exchanged(along_z, act):
        @pl.when(s < BY_CHUNK)
        def _():
            for k in ORDER:
                for c in range(NC):
                    act(grad_copy(pl.ds(c * rows_c, rows_c), c, along_z, k))

        @pl.when(s >= BY_CHUNK)
        def _():
            for k in ORDER:
                act(grad_copy(pl.ds(0, length), 0, along_z, k))

    def end_copy(along_z, k):
        return spread_copy(
            lambda there: parts.at[int(not along_z), there], ends.at[int(not along_z), k - 1],
            esend.at[int(not along_z)], erecv.at[int(not along_z)], along_z, k,
        )

    for k in ORDER:
        for along_z in (False, True):
            mix_copy(along_z, k).start()

    def mix_end():
        for k in ORDER:
            for along_z in (False, True):
                mix_copy(along_z, k).wait_send()

    for copy in unsent:
        copy.wait_send()

    @pl.when(s < 2)
    def _():
        mix_end()

    @pl.when(s < SECTIONS - 1)
    def _():
        turn_weights(0)

    for c in range(1, NC):
        turn_weights(c)
    for p in range(PAIRS):
        cols = slice(p * PAIR, (p + 1) * PAIR)
        ktb[cols] = (kb[:, cols] * HEAD_DIM ** (-0.5)).T

    for c in reversed(range(NC)):
        lo, hi = c * rows_c, (c + 1) * rows_c

        @pl.when(s < SECTIONS - 1)
        def _():
            backward_copy(c).wait_recv()

        @pl.when(s > 0)
        def _():
            g = gin[lo:hi]
            dmb[...] = dot(g, weight(3), NN).astype(jnp.bfloat16)
            for p in range(PAIRS):
                cols = slice(p * PAIR, (p + 1) * PAIR)
                d01 = wide_halves(dmb[:, cols], low)
                turned = ptb[c, p, :hi]
                wide = turned.astype(jnp.float32)
                dweights = dot(vb[:hi, cols], d01, NT)
                delta = jnp.sum(wide * dweights, axis=0, keepdims=True)
                dsb[p, :hi] = (wide * (dweights - delta)).astype(jnp.bfloat16)
                dvalues = dot(turned, d01, NN)
                dvb[:hi, cols] = dvalues if c == NC - 1 else dvb[:hi, cols] + dvalues
            for p in range(PAIRS):
                cols = slice(p * PAIR, (p + 1) * PAIR)
                dq01 = dot(ktb[cols, :hi], dsb[p, :hi], NN)
                dqb[cols] = jnp.where(low_rows, dq01[:, :WIDE], dq01[:, WIDE:]).astype(jnp.bfloat16)
                dkeys = dot(dsb[p, :hi], wide_halves(qb[lo:hi, cols], low), NN)
                dkb[:hi, cols] = dkeys if c == NC - 1 else dkb[:hi, cols] + dkeys
            dn = dot(dqb[...], weight(0), TN)[:rows_c]
            dn += dot(dkb[lo:hi].astype(jnp.bfloat16), weight(1), NN)
            dn += dot(dvb[lo:hi].astype(jnp.bfloat16), weight(2), NN)
            h = hid[lo:hi].astype(jnp.float32)
            r = lax.rsqrt(jnp.mean(h * h, axis=-1, keepdims=True) + epsilon)
            along = jnp.mean(dn * h, axis=-1, keepdims=True)
            dh = dn * r - h * (r * r * r * along)
            gout[lo:hi] = (g.astype(jnp.float32) + dh).astype(jnp.bfloat16)
            backward_copy(c).start()

        @pl.when(s < BY_CHUNK)
        def _():
            exchange(pl.ds(lo, rows_c), c)

    @pl.when(s >= BY_CHUNK)
    def _():
        exchange(pl.ds(0, length), 0)

    for along_z in (False, True):
        i, me, source = int(along_z), (z if along_z else y), (gswap if along_z else gin)
        mixes[i, 0] = mixb[:, i * half : (i + 1) * half]
        gs[i, 0] = source[:, pl.ds(pl.multiple_of(me * slice_cols, slice_cols), slice_cols)]
        for k in ORDER:
            mix_copy(along_z, k).wait_recv()
        exchanged(along_z, lambda copy: copy.wait_recv())
        total = dot(
            gs[i].reshape(RING * length, slice_cols), mixes[i].reshape(RING * length, half), TN
        )
        parts[i] = total.astype(jnp.bfloat16).reshape(RING, own, half)
        for k in ORDER:
            end_copy(not along_z, k).start()
    for along_z in (False, True):
        exchanged(along_z, lambda copy: copy.wait_send())

    @pl.when(s >= 2)
    def _():
        mix_end()

    for along_z in (False, True):
        i, me = int(along_z), (y if along_z else z)
        total = parts[i, me].astype(jnp.float32)
        for k in ORDER:
            end_copy(not along_z, k).wait_recv()
            total += ends[i, k - 1].astype(jnp.float32)
        o_ref[:, i * half : (i + 1) * half] = total

    for along_z in (False, True):
        for k in ORDER:
            end_copy(along_z, k).wait_send()
    for c in range(NC):
        @pl.when(s < SECTIONS - 1)
        def _():
            forward_copy(c).wait_send()

        @pl.when(s > 0)
        def _():
            backward_copy(c).wait_send()


def local(hidden_in, cotangent, segments, attn_weights, out_weight):
    length, width = hidden_in.shape[1:]
    own = out_weight.shape[1]
    rows_c = length // NC
    half = width // 2
    full = pltpu.VMEM((length, width), jnp.bfloat16)
    dma = lambda *shape: pltpu.SemaphoreType.DMA(shape)
    anywhere = pl.BlockSpec(memory_space=pl.ANY)
    result = pl.pallas_call(
        pipeline_kernel,
        name="pipeline",
        out_shape=jax.ShapeDtypeStruct((own, width), jnp.float32),
        in_specs=[anywhere, anywhere, pl.BlockSpec(memory_space=pltpu.VMEM), anywhere, anywhere],
        out_specs=pl.BlockSpec(memory_space=pltpu.VMEM),
        scratch_shapes=[
            pltpu.VMEM((4, RING, RING, own, width), jnp.bfloat16),
            pltpu.VMEM((length, length), jnp.float32),
            pltpu.VMEM((width, width), jnp.bfloat16),
            full,
            pltpu.VMEM((2, RING, length, half), jnp.bfloat16),
            pltpu.VMEM((2, RING, length, width // RING), jnp.bfloat16),
            pltpu.VMEM((2, RING, own, half), jnp.bfloat16),
            pltpu.VMEM((2, RING - 1, own, half), jnp.bfloat16),
            dma(2, 2, 4), dma(2, 2, 4), dma(2, 9, 2, 4), dma(2, 9, 2, 4),
            dma(2, RING - 1), dma(2, RING - 1), dma(2, NC, RING - 1), dma(2, NC, RING - 1),
            dma(2, RING - 1), dma(2, RING - 1), dma(5), pltpu.SemaphoreType.REGULAR,
        ] + [full] * 5 + [pltpu.VMEM((2 * WIDE, width), jnp.bfloat16), full, full] + [
            pltpu.VMEM((NC, PAIRS, 2 * WIDE, 2 * WIDE), jnp.bfloat16),
            pltpu.VMEM((NC, PAIRS, 2 * WIDE, 2 * WIDE), jnp.bfloat16),
            pltpu.VMEM((width, 2 * WIDE), jnp.bfloat16),
            pltpu.VMEM((PAIRS, length, 2 * WIDE), jnp.bfloat16),
            pltpu.VMEM((4, width, width), jnp.bfloat16),
            pltpu.VMEM((rows_c, width), jnp.bfloat16),
            pltpu.VMEM((width, WIDE), jnp.bfloat16),
            pltpu.VMEM((length, width), jnp.float32),
            pltpu.VMEM((length, width), jnp.float32),
        ] + [dma(NC)] * 4,
        compiler_params=pltpu.CompilerParams(
            collective_id=1, has_side_effects=True, vmem_limit_bytes=56 << 20
        ),
    )(hidden_in[0], cotangent[0], segments, attn_weights[0], out_weight[0])
    return result[None]


def solution(mesh):
    in_specs = (
        P("dp", None, None),
        P("dp", None, None),
        P("dp", None),
        P("section", None, "dp", None),
        P("section", "dp", None),
    )
    return jax.shard_map(
        local, mesh=mesh, in_specs=in_specs, out_specs=P("section", "dp", None), check_vma=False
    )
```

```python
import functools
import jax
import jax.numpy as jnp
from jax import lax
from jax.experimental import pallas as pl
from jax.experimental.pallas import tpu as pltpu
from jax.sharding import PartitionSpec as P

MESH = pl.DeviceIdType.MESH
HEADS = 16
HEAD_DIM = 64
PAIRS = HEADS // 2
PAIR = 2 * HEAD_DIM
WIDE = 128
NC = 2
BY_CHUNK = 2
LATE = 6
SECTIONS = 8
RING = 8
epsilon = 1e-05
masked_score = -1e30

NT = (((1,), (1,)), ((), ()))
NN = (((1,), (0,)), ((), ()))
TN = (((0,), (0,)), ((), ()))


def dot(a, b, dims):
    return lax.dot_general(a, b, dims, preferred_element_type=jnp.float32)


def halves(block, low):
    zero = jnp.zeros_like(block)
    return jnp.concatenate([jnp.where(low, block, zero), jnp.where(low, zero, block)], axis=0)


def first_steps(kind, way):
    return RING // 2 if (way == 1) == (kind == 0) else RING // 2 - 1


def second_steps(a, way):
    return RING // 2 if (way == 1) == (a % 2 == 0) else RING // 2 - 1


def place():
    d = lax.axis_index("dp")
    return d // RING, lax.rem(d, RING)


def around(me, step):
    return lax.rem(me + step + 2 * RING, RING)


def block_copy(w_ref, kind, y, z, other, send, recv):
    ref = w_ref.at[2 * kind : 2 * kind + 2, y, z]
    return pltpu.make_async_remote_copy(
        src_ref=ref, dst_ref=ref, send_sem=send, recv_sem=recv, device_id={"dp": other}, device_id_type=MESH
    )


def first_copy(w_ref, sends, recvs, kind, way, step):
    y, z = place()
    sems = sends.at[kind, (1 - way) // 2, step - 1], recvs.at[kind, (1 - way) // 2, step - 1]
    if kind == 0:
        return block_copy(w_ref, kind, y, around(z, -way * (step - 1)), y * RING + around(z, way), *sems)
    return block_copy(w_ref, kind, around(y, -way * (step - 1)), z, around(y, way) * RING + z, *sems)


def second_copy(w_ref, sends, recvs, kind, a, way, step):
    y, z = place()
    sems = sends.at[kind, a + 4, (1 - way) // 2, step - 1], recvs.at[kind, a + 4, (1 - way) // 2, step - 1]
    if kind == 0:
        return block_copy(
            w_ref, kind, around(y, -way * (step - 1)), around(z, a), around(y, way) * RING + z, *sems
        )
    return block_copy(w_ref, kind, around(y, a), around(z, -way * (step - 1)), y * RING + around(z, way), *sems)


def offsets(kind):
    return [0, -1, 1, -2, 2, -3, 3, 4 if kind == 1 else -4]


WAYS = (1, -1)


LIMIT = 6
TURN = 2


def gather(w_ref, send1, recv1, send2, recv2, beside, give_turn):
    first = functools.partial(first_copy, w_ref, send1, recv1)
    second = functools.partial(second_copy, w_ref, send2, recv2)
    under_way = {(axis, way): [] for axis in range(2) for way in WAYS}

    def start(axis, way, copy):
        queue = under_way[axis, way]
        if len(queue) == LIMIT:
            queue.pop(0).wait_send()
        copy.start()
        queue.append(copy)

    for kind in range(2):
        for way in WAYS:
            start(kind, way, first(kind, way, 1))
    for kind in range(2):
        for way in WAYS:
            start(1 - kind, way, second(kind, 0, way, 1))
    for wave in range(1, RING + 1):
        for kind in range(2):
            for way in WAYS:
                if wave <= first_steps(kind, way):
                    first(kind, way, wave).wait_recv()
                    if wave < first_steps(kind, way):
                        start(kind, way, first(kind, way, wave + 1))
                    for onward in WAYS:
                        start(1 - kind, onward, second(kind, -way * wave, onward, 1))
        for a_index in FAR:
            for kind in range(2):
                a = offsets(kind)[a_index]
                step = wave - abs(a)
                for way in WAYS:
                    if 1 <= step <= second_steps(a, way):
                        second(kind, a, way, step).wait_recv()
                        if step < second_steps(a, way):
                            start(1 - kind, way, second(kind, a, way, step + 1))
        beside(wave)
        if wave == TURN:
            give_turn()
    return [copy for queue in under_way.values() for copy in queue]


FAR = tuple(reversed(range(RING)))


ORDER = (4, 3, 5, 2, 6, 1, 7)


def spread_copy(src, dst, send, recv, along_z, k):
    y, z = place()
    there = around(z if along_z else y, k)
    other = y * RING + there if along_z else there * RING + z
    return pltpu.make_async_remote_copy(
        src_ref=src(there), dst_ref=dst, send_sem=send.at[k - 1], recv_sem=recv.at[k - 1],
        device_id={"dp": other}, device_id_type=MESH,
    )


def wide_halves(block, low):
    zero = jnp.zeros_like(block)
    gap = jnp.zeros((WIDE - block.shape[0], block.shape[1]), block.dtype)
    return jnp.concatenate([jnp.where(low, block, zero), gap, jnp.where(low, zero, block), gap], axis=0)


def pipeline_kernel(
    x_ref, cot_ref, seg_ref, attn_ref, out_ref, o_ref,
    w_ref, bias_ref, swap, gswap, mixes, gs, parts, ends,
    gsend1, grecv1, gsend2, grecv2, msend, mrecv, csend, crecv, esend, erecv, lsem, turn,
    hid, outb, gin, gout, qb, kb, vb, mixb, pb, ptb, ktb, dsb, wtb, dmb, dqb, dkb, dvb,
    fsend, frecv, bsend, brecv,
):
    s = lax.axis_index("section")
    y, z = place()
    length, width = x_ref.shape
    rows_c = length // NC
    half = width // 2
    slice_cols = width // RING
    barrier = pltpu.get_barrier_semaphore()
    for step in (1, SECTIONS - 1):
        other = lax.rem(s + step, SECTIONS)
        pl.semaphore_signal(barrier, inc=1, device_id={"section": other}, device_id_type=MESH)
    for step in range(1, RING):
        for other in (around(y, step) * RING + z, y * RING + around(z, step)):
            pl.semaphore_signal(barrier, inc=1, device_id={"dp": other}, device_id_type=MESH)
    shard = [pltpu.make_async_copy(attn_ref.at[j], w_ref.at[j, y, z], lsem.at[j]) for j in range(3)]
    shard.append(pltpu.make_async_copy(out_ref, w_ref.at[3, y, z], lsem.at[3]))
    for copy in shard:
        copy.start()
    in_copy = pltpu.make_async_copy(x_ref, hid, lsem.at[4])
    cot_copy = pltpu.make_async_copy(cot_ref, gin, lsem.at[4])

    @pl.when(s == 0)
    def _():
        in_copy.start()

    @pl.when(s == SECTIONS - 1)
    def _():
        cot_copy.start()

    for copy in shard:
        copy.wait()
    pl.semaphore_wait(barrier, 2 + 2 * (RING - 1))
    own = slice_cols // RING

    def mask():
        ids = lax.broadcasted_iota(jnp.int32, (32, length), 0)
        one_hot = jnp.where(ids == seg_ref[...], 1.0, 0.0).astype(jnp.bfloat16)
        same = dot(one_hot, one_hot, TN) > 0.5
        query = lax.broadcasted_iota(jnp.int32, (length, length), 0)
        key = lax.broadcasted_iota(jnp.int32, (length, length), 1)
        any_segment = lax.broadcast(lax.rem(s, 2), (length, length)) == 1
        allowed = (key <= query) & (same | any_segment)
        bias_ref[...] = jnp.where(allowed, 0.0, masked_score)
        pb[...] = jnp.zeros_like(pb)
        kb[length:] = jnp.zeros((kb.shape[0] - length, width), kb.dtype)

    def swap_rows(j):
        row = lax.broadcasted_iota(jnp.int32, (slice_cols, width), 0) + j * slice_cols
        col = lax.broadcasted_iota(jnp.int32, (slice_cols, width), 1)
        source = lax.rem(col, slice_cols) // own * slice_cols + col // slice_cols * own + lax.rem(col, own)
        swap[j * slice_cols : (j + 1) * slice_cols] = jnp.where(row == source, 1.0, 0.0).astype(jnp.bfloat16)

    def beside(wave):
        swap_rows(wave - 1)
        if wave == 4:
            mask()

    lead = lax.rem(s, 2) == 0

    def give_turn():
        @pl.when(lead)
        def _():
            pl.semaphore_signal(turn, inc=1, device_id={"section": s + 1 - 2 * lax.rem(s, 2)}, device_id_type=MESH)

    @pl.when(jnp.logical_not(lead))
    def _():
        pl.semaphore_wait(turn, 1)

    unsent = gather(w_ref, gsend1, grecv1, gsend2, grecv2, beside, give_turn)

    @pl.when(s == 0)
    def _():
        in_copy.wait()

    @pl.when(s == SECTIONS - 1)
    def _():
        cot_copy.wait()

    weight = lambda j: w_ref[j].reshape(width, width)

    def forward_copy(c):
        rows = pl.ds(c * rows_c, rows_c)
        return pltpu.make_async_remote_copy(
            src_ref=outb.at[rows], dst_ref=hid.at[rows], send_sem=fsend.at[c], recv_sem=frecv.at[c],
            device_id={"section": jnp.minimum(s + 1, SECTIONS - 1)}, device_id_type=MESH,
        )

    def backward_copy(c):
        rows = pl.ds(c * rows_c, rows_c)
        return pltpu.make_async_remote_copy(
            src_ref=gout.at[rows], dst_ref=gin.at[rows], send_sem=bsend.at[c], recv_sem=brecv.at[c],
            device_id={"section": jnp.maximum(s - 1, 0)}, device_id_type=MESH,
        )

    def mix_copy(rows, c, along_z, k):
        cols = pl.ds(half if along_z else 0, half)
        return spread_copy(
            lambda there: mixb.at[rows, cols], mixes.at[int(along_z), k, rows], msend.at[int(along_z), c],
            mrecv.at[int(along_z), c], along_z, k,
        )

    def mix_each(rows, c, act):
        for k in ORDER:
            for along_z in (False, True):
                act(mix_copy(rows, c, along_z, k))

    def mix_all(act):
        @pl.when(s < LATE)
        def _():
            mix_each(pl.ds(0, length), 0, act)

        @pl.when(s >= LATE)
        def _():
            for c in range(NC):
                mix_each(pl.ds(c * rows_c, rows_c), c, act)

    def turn_weights(c):
        for p in range(PAIRS):
            ptb[c, p] = pb[c, p].T

    low_rows = lax.broadcasted_iota(jnp.int32, (PAIR, WIDE), 0) < HEAD_DIM
    low = lax.broadcasted_iota(jnp.int32, (rows_c, PAIR), 1) < HEAD_DIM

    for j in range(4):
        for i in range(RING):
            block = w_ref[j, i].reshape(slice_cols, width)
            wtb[j, :, i * slice_cols : (i + 1) * slice_cols] = block.T

    for c in range(NC):
        lo, hi = c * rows_c, (c + 1) * rows_c

        @pl.when(s > 0)
        def _():
            forward_copy(c).wait_recv()

        h = hid[lo:hi].astype(jnp.float32)
        r = lax.rsqrt(jnp.mean(h * h, axis=-1, keepdims=True) + epsilon)
        normed = (h * r).astype(jnp.bfloat16)
        qb[lo:hi] = (dot(normed, wtb[0], NN) * HEAD_DIM ** (-0.5)).astype(jnp.bfloat16)
        kb[lo:hi] = dot(normed, wtb[1], NN).astype(jnp.bfloat16)
        bias = bias_ref[lo:hi, :hi]
        bias2 = jnp.concatenate([bias, bias], axis=0)
        for p in range(PAIRS):
            cols = slice(p * PAIR, (p + 1) * PAIR)
            q01 = halves(qb[lo:hi, cols], low)
            scores = dot(q01, kb[:hi, cols], NT) + bias2
            top = jnp.max(scores, axis=-1, keepdims=True)
            e = jnp.exp(scores - top)
            weights = (e * (1.0 / jnp.sum(e, axis=-1, keepdims=True))).astype(jnp.bfloat16)
            pb[c, p, :rows_c, :hi] = weights[:rows_c]
            pb[c, p, WIDE : WIDE + rows_c, :hi] = weights[rows_c:]
            if p % 2 == 0:
                two = slice(p * PAIR, (p + 2) * PAIR)
                vb[lo:hi, two] = dot(normed, wtb[2, :, two], NN).astype(jnp.bfloat16)
        for p in range(PAIRS):
            cols = slice(p * PAIR, (p + 1) * PAIR)
            o = dot(pb[c, p, :, :hi], vb[:hi, cols], NN)
            mixb[lo:hi, cols] = jnp.where(low, o[:rows_c], o[WIDE : WIDE + rows_c]).astype(jnp.bfloat16)

        @pl.when(s < SECTIONS - 1)
        def _():
            added = hid[lo:hi].astype(jnp.float32) + dot(mixb[lo:hi], wtb[3], NN)
            outb[lo:hi] = added.astype(jnp.bfloat16)
            forward_copy(c).start()

        @pl.when(s >= LATE)
        def _():
            mix_each(pl.ds(lo, rows_c), c, lambda copy: copy.start())

        if c == 0:
            @pl.when(s == SECTIONS - 1)
            def _():
                turn_weights(0)

    def grad_copy(rows, c, along_z, k):
        source = gswap if along_z else gin
        return spread_copy(
            lambda there: source.at[rows, pl.ds(pl.multiple_of(there * slice_cols, slice_cols), slice_cols)],
            gs.at[int(along_z), k, rows], csend.at[int(along_z), c], crecv.at[int(along_z), c], along_z, k,
        )

    def exchange(rows, c):
        for k in ORDER:
            grad_copy(rows, c, False, k).start()
        gswap[rows] = dot(gin[rows], swap[...], NN).astype(jnp.bfloat16)
        for k in ORDER:
            grad_copy(rows, c, True, k).start()

    def exchanged(along_z, act):
        @pl.when(s < BY_CHUNK)
        def _():
            for k in ORDER:
                for c in range(NC):
                    act(grad_copy(pl.ds(c * rows_c, rows_c), c, along_z, k))

        @pl.when(s >= BY_CHUNK)
        def _():
            for k in ORDER:
                act(grad_copy(pl.ds(0, length), 0, along_z, k))

    def end_copy(along_z, k):
        return spread_copy(
            lambda there: parts.at[int(not along_z), there], ends.at[int(not along_z), k - 1],
            esend.at[int(not along_z)], erecv.at[int(not along_z)], along_z, k,
        )

    @pl.when(s < LATE)
    def _():
        mix_each(pl.ds(0, length), 0, lambda copy: copy.start())

    def mix_end():
        mix_all(lambda copy: copy.wait_send())

    for copy in unsent:
        copy.wait_send()

    def mix_received():
        mix_all(lambda copy: copy.wait_recv())

    @pl.when(s < 2)
    def _():
        mix_end()
        mix_received()

    @pl.when(s < SECTIONS - 1)
    def _():
        turn_weights(0)

    for c in range(1, NC):
        turn_weights(c)
    for p in range(PAIRS):
        cols = slice(p * PAIR, (p + 1) * PAIR)
        ktb[cols] = (kb[:, cols] * HEAD_DIM ** (-0.5)).T

    for c in reversed(range(NC)):
        lo, hi = c * rows_c, (c + 1) * rows_c

        @pl.when(s < SECTIONS - 1)
        def _():
            backward_copy(c).wait_recv()

        @pl.when(s > 0)
        def _():
            g = gin[lo:hi]
            dmb[...] = dot(g, weight(3), NN).astype(jnp.bfloat16)
            for p in range(PAIRS):
                cols = slice(p * PAIR, (p + 1) * PAIR)
                d01 = wide_halves(dmb[:, cols], low)
                turned = ptb[c, p, :hi]
                wide = turned.astype(jnp.float32)
                dweights = dot(vb[:hi, cols], d01, NT)
                delta = jnp.sum(wide * dweights, axis=0, keepdims=True)
                dsb[p, :hi] = (wide * (dweights - delta)).astype(jnp.bfloat16)
                dvalues = dot(turned, d01, NN)
                dvb[:hi, cols] = dvalues if c == NC - 1 else dvb[:hi, cols] + dvalues
            for p in range(PAIRS):
                cols = slice(p * PAIR, (p + 1) * PAIR)
                dq01 = dot(ktb[cols, :hi], dsb[p, :hi], NN)
                dqb[cols] = jnp.where(low_rows, dq01[:, :WIDE], dq01[:, WIDE:]).astype(jnp.bfloat16)
                dkeys = dot(dsb[p, :hi], wide_halves(qb[lo:hi, cols], low), NN)
                dkb[:hi, cols] = dkeys if c == NC - 1 else dkb[:hi, cols] + dkeys
            dn = dot(dqb[...], weight(0), TN)[:rows_c]
            dn += dot(dkb[lo:hi].astype(jnp.bfloat16), weight(1), NN)
            dn += dot(dvb[lo:hi].astype(jnp.bfloat16), weight(2), NN)
            h = hid[lo:hi].astype(jnp.float32)
            r = lax.rsqrt(jnp.mean(h * h, axis=-1, keepdims=True) + epsilon)
            along = jnp.mean(dn * h, axis=-1, keepdims=True)
            dh = dn * r - h * (r * r * r * along)
            gout[lo:hi] = (g.astype(jnp.float32) + dh).astype(jnp.bfloat16)
            backward_copy(c).start()

        @pl.when(s < BY_CHUNK)
        def _():
            exchange(pl.ds(lo, rows_c), c)

    @pl.when(s >= BY_CHUNK)
    def _():
        exchange(pl.ds(0, length), 0)

    @pl.when(s >= 2)
    def _():
        mix_received()

    for along_z in (False, True):
        i, me, source = int(along_z), (z if along_z else y), (gswap if along_z else gin)
        mixes[i, 0] = mixb[:, i * half : (i + 1) * half]
        gs[i, 0] = source[:, pl.ds(pl.multiple_of(me * slice_cols, slice_cols), slice_cols)]
        exchanged(along_z, lambda copy: copy.wait_recv())
        total = dot(
            gs[i].reshape(RING * length, slice_cols), mixes[i].reshape(RING * length, half), TN
        )
        parts[i] = total.astype(jnp.bfloat16).reshape(RING, own, half)
        for k in ORDER:
            end_copy(not along_z, k).start()
    for along_z in (False, True):
        exchanged(along_z, lambda copy: copy.wait_send())

    @pl.when(s >= 2)
    def _():
        mix_end()

    for along_z in (False, True):
        i, me = int(along_z), (y if along_z else z)
        total = parts[i, me].astype(jnp.float32)
        for k in ORDER:
            end_copy(not along_z, k).wait_recv()
            total += ends[i, k - 1].astype(jnp.float32)
        o_ref[:, i * half : (i + 1) * half] = total

    for along_z in (False, True):
        for k in ORDER:
            end_copy(along_z, k).wait_send()
    for c in range(NC):
        @pl.when(s < SECTIONS - 1)
        def _():
            forward_copy(c).wait_send()

        @pl.when(s > 0)
        def _():
            backward_copy(c).wait_send()


def local(hidden_in, cotangent, segments, attn_weights, out_weight):
    length, width = hidden_in.shape[1:]
    own = out_weight.shape[1]
    rows_c = length // NC
    half = width // 2
    full = pltpu.VMEM((length, width), jnp.bfloat16)
    dma = lambda *shape: pltpu.SemaphoreType.DMA(shape)
    anywhere = pl.BlockSpec(memory_space=pl.ANY)
    result = pl.pallas_call(
        pipeline_kernel,
        name="pipeline",
        out_shape=jax.ShapeDtypeStruct((own, width), jnp.float32),
        in_specs=[anywhere, anywhere, pl.BlockSpec(memory_space=pltpu.VMEM), anywhere, anywhere],
        out_specs=pl.BlockSpec(memory_space=pltpu.VMEM),
        scratch_shapes=[
            pltpu.VMEM((4, RING, RING, own, width), jnp.bfloat16),
            pltpu.VMEM((length, length), jnp.float32),
            pltpu.VMEM((width, width), jnp.bfloat16),
            full,
            pltpu.VMEM((2, RING, length, half), jnp.bfloat16),
            pltpu.VMEM((2, RING, length, width // RING), jnp.bfloat16),
            pltpu.VMEM((2, RING, own, half), jnp.bfloat16),
            pltpu.VMEM((2, RING - 1, own, half), jnp.bfloat16),
            dma(2, 2, 4), dma(2, 2, 4), dma(2, 9, 2, 4), dma(2, 9, 2, 4),
            dma(2, NC, RING - 1), dma(2, NC, RING - 1), dma(2, NC, RING - 1), dma(2, NC, RING - 1),
            dma(2, RING - 1), dma(2, RING - 1), dma(5), pltpu.SemaphoreType.REGULAR,
        ] + [full] * 5 + [pltpu.VMEM((2 * WIDE, width), jnp.bfloat16), full, full] + [
            pltpu.VMEM((NC, PAIRS, 2 * WIDE, 2 * WIDE), jnp.bfloat16),
            pltpu.VMEM((NC, PAIRS, 2 * WIDE, 2 * WIDE), jnp.bfloat16),
            pltpu.VMEM((width, 2 * WIDE), jnp.bfloat16),
            pltpu.VMEM((PAIRS, length, 2 * WIDE), jnp.bfloat16),
            pltpu.VMEM((4, width, width), jnp.bfloat16),
            pltpu.VMEM((rows_c, width), jnp.bfloat16),
            pltpu.VMEM((width, WIDE), jnp.bfloat16),
            pltpu.VMEM((length, width), jnp.float32),
            pltpu.VMEM((length, width), jnp.float32),
        ] + [dma(NC)] * 4,
        compiler_params=pltpu.CompilerParams(
            collective_id=1, has_side_effects=True, vmem_limit_bytes=56 << 20
        ),
    )(hidden_in[0], cotangent[0], segments, attn_weights[0], out_weight[0])
    return result[None]


def solution(mesh):
    in_specs = (
        P("dp", None, None),
        P("dp", None, None),
        P("dp", None),
        P("section", None, "dp", None),
        P("section", "dp", None),
    )
    return jax.shard_map(
        local, mesh=mesh, in_specs=in_specs, out_specs=P("section", "dp", None), check_vma=False
    )
```
